512 devices in a mesh: dp: 32 (over y_hi, z), ctx: 16 (over y_lo, x, core).
Axes of the slice: x: 4, y: 4 (y_hi: 2, y_lo: 2; y = y_hi * 2 + y_lo), z: 16, core: 2. Of those that a mesh axis runs over, the one named last changes fastest.
Arguments:
- bases: int32 [32, 163840], P('dp', 'ctx'), may hold values from 0 to 3
- embed_w: bfloat16 [512, 1536], replicated, may hold values from -0.5 to 0.5
- conv_w: bfloat16 [5, 1536, 1536], P(None, None, 'ctx'), may hold values from -0.0625 to 0.0625
- conv_b: float32 [1536], P('ctx'), may hold values from -3 to 3
- norm_g: float32 [1536], replicated, may hold values from 0.1 to 1.9
- qkv_w: bfloat16 [1536, 3072], P(None, 'ctx'), may hold values from -1 to 1
- wo: bfloat16 [1024, 1536], P('ctx'), may hold values from -1.5 to 1.5
- cotangent: bfloat16 [32, 1280, 1536], P('dp', 'ctx'), may hold values from -0.59765625 to 0.59765625
Outputs:
- layer_out: bfloat16 [32, 1280, 1536], P('dp', 'ctx')
- wo_grad: bfloat16 [1024, 1536], P('ctx')
The draws below stay inside these ranges and needn't reach their ends.
All inputs are finite; a program needn't handle non-finite values.
Results may differ from the reference program's by a relative error of at most 0.024.
Values may be sent and summed in bfloat16 or wider, within the bound.
A program may use at most 64 MiB of HBM per device.

```python
import jax
import jax.numpy as jnp
from jax import lax

D = 1536
DH = 64
KW = 5
PATCH = 128
SEQS = 32
HEADS = 16
LEN = 1280


def draw_qkv_w(key, part):
    key = jax.random.fold_in(key, 11)
    first_key = jax.random.fold_in(key, 0)
    full_draw = jax.random.normal(first_key, (D, HEADS, 3, DH), jnp.float32) * D ** (-0.5)
    return jnp.clip(full_draw, -1.0, 1.0).reshape(D, HEADS * 3 * DH).astype(jnp.bfloat16)


def plant(drawn, key, smallest, high):
    longest = drawn.shape.index(max(drawn.shape))
    spots = []
    for shift in (0, 1):
        where = [jax.random.randint(jax.random.fold_in(key, axis), (), 0, length) for axis, length in enumerate(drawn.shape)]
        where[longest] = (where[longest] + shift) % drawn.shape[longest]
        spots.append(tuple(where))
    return drawn.at[spots[0]].set(smallest).at[spots[1]].set(high)


def level_of(rng, extent, pieces, least, largest):
    factor_of = 1.0
    for axis_at, shards_of in pieces:
        steps = jax.random.uniform(jax.random.fold_in(jax.random.fold_in(rng, 6), axis_at), (shards_of,), jnp.float32, least / len(pieces), largest / len(pieces))
        factor_of = factor_of * jnp.repeat(jnp.exp(steps), extent[axis_at] // shards_of).reshape((-1,) + (1,) * (len(extent) - 1 - axis_at))
    return factor_of


def gaussian(rng, shape, scale, most, cuts=(), kind=jnp.bfloat16):
    values = jax.random.normal(rng, shape, jnp.float32) * scale
    if len(cuts) > 0:
        values = level_of(rng, shape, cuts, -0.22, 0.18) * values
    return jnp.clip(values, min=-most, max=most).astype(kind)


def setup_inputs(seed: int = 0) -> dict:
    arg_keys = jax.random.split(jax.random.key(seed), 9)
    bases = plant(jax.random.randint(arg_keys[0], (SEQS, LEN * PATCH), 0, 4), jax.random.fold_in(arg_keys[0], 1), 0, 3).astype(jnp.int32)
    embed_w = gaussian(arg_keys[1], (4 * PATCH, D), PATCH ** -0.5, 0.5)
    conv_w = gaussian(arg_keys[2], (KW, D, D), (KW * D) ** -0.5, 0.0625, ((2, 16),))
    conv_b = gaussian(arg_keys[3], (D,), 0.5, 3.0, ((0, 16),), jnp.float32)
    norm_g = jnp.clip(1.0 + 0.18 * jax.random.normal(arg_keys[4], (D,), jnp.float32), 0.1, 1.9)
    qkv_w = draw_qkv_w(jax.random.fold_in(arg_keys[8], 71), 0)
    wo = gaussian(arg_keys[6], (HEADS * DH, D), (DH // 4) ** -0.5, 1.5, ((0, 16),))
    cotangent = gaussian(arg_keys[7], (SEQS, LEN, D), 0.1, 0.59765625, ((0, 32), (1, 16)))
    return dict(bases=bases, embed_w=embed_w, conv_w=conv_w, conv_b=conv_b, norm_g=norm_g, qkv_w=qkv_w, wo=wo, cotangent=cotangent)


def patch_embed(seq_bases, embed_w):
    grouped = seq_bases.reshape(-1, PATCH)
    onehot = (grouped[:, :, None] == jnp.arange(4, dtype=jnp.int32)[None, None, :]).astype(jnp.bfloat16)
    onehot = onehot.reshape(grouped.shape[0], PATCH * 4)
    return jnp.dot(onehot, embed_w, preferred_element_type=jnp.float32).astype(jnp.bfloat16)

def conv_section(embedded, conv_w, conv_b):
    half_kernel = KW // 2
    seq_rows = embedded.shape[0]
    padded = jnp.pad(embedded, ((half_kernel, half_kernel), (0, 0)))
    pre_act = jnp.zeros((seq_rows, conv_w.shape[2]), jnp.float32) + conv_b[None, :]
    for tap_index in range(KW):
        pre_act = pre_act + jnp.dot(padded[tap_index:tap_index + seq_rows], conv_w[tap_index], preferred_element_type=jnp.float32)
    return (embedded.astype(jnp.float32) + jax.nn.gelu(pre_act)).astype(jnp.bfloat16)

def rms_norm(stream, norm_g):
    values = stream.astype(jnp.float32)
    rescale = lax.rsqrt(lax.optimization_barrier(jnp.mean(values * values, axis=-1, keepdims=True)) + 1e-06)
    return (values * rescale * norm_g[None, :]).astype(jnp.bfloat16)

def attend(head_proj, head_size):
    query_rows = head_proj[:, :head_size]
    key_rows = head_proj[:, head_size:2 * head_size]
    value_rows = head_proj[:, 2 * head_size:]
    scores = jnp.dot(query_rows, key_rows.T, preferred_element_type=jnp.float32) * head_size ** (-0.5)
    row_peak = lax.optimization_barrier(jnp.max(scores, axis=1, keepdims=True))
    exponent = jnp.exp(scores - row_peak)
    weights = (exponent / lax.optimization_barrier(jnp.sum(exponent, axis=1, keepdims=True))).astype(jnp.bfloat16)
    return jnp.dot(weights, value_rows, preferred_element_type=jnp.float32).astype(jnp.bfloat16)

def reference(bases, embed_w, conv_w, conv_b, norm_g, qkv_w, wo, cotangent):
    wo_heads = wo.reshape(HEADS, DH, D)

    def one_sequence(running, inputs):
        seq_bases, seq_cot = inputs
        embedded = patch_embed(seq_bases, embed_w)
        stream = conv_section(embedded, conv_w, conv_b)
        normed = rms_norm(stream, norm_g)
        projected = jnp.dot(normed, qkv_w, preferred_element_type=jnp.float32).astype(jnp.bfloat16)
        per_head = jnp.transpose(projected.reshape(LEN, HEADS, 3 * DH), (1, 0, 2))

        def one_head(head_pair):
            head_proj, head_out = head_pair
            attended = attend(head_proj, DH)
            head_term = jnp.dot(attended, head_out, preferred_element_type=jnp.float32).astype(jnp.bfloat16)
            return (attended, head_term)
        attended, head_terms = lax.map(one_head, (per_head, wo_heads))
        layer_rows = (stream.astype(jnp.float32) + lax.optimization_barrier(jnp.sum(head_terms.astype(jnp.float32), axis=0))).astype(jnp.bfloat16)
        seq_grad = jnp.einsum('htk,td->hkd', attended.astype(jnp.float32), seq_cot.astype(jnp.float32), precision=lax.Precision.HIGHEST)
        return (running + seq_grad.reshape(HEADS * DH, D), layer_rows)
    zero_grad = jnp.zeros((HEADS * DH, D), jnp.float32)
    grad_sum, layer_out = lax.scan(one_sequence, zero_grad, (bases, cotangent))
    return (layer_out, grad_sum.astype(jnp.bfloat16))
```

```python
import functools

import jax
import jax.numpy as jnp
from jax import lax
from jax.experimental import pallas as pl
from jax.experimental.pallas import tpu as pltpu
from jax.sharding import PartitionSpec as P

MESH = pl.DeviceIdType.MESH
BF = jnp.bfloat16
F32 = jnp.float32
LA = 384


def _al(v, m):
    return pl.multiple_of(v, m)


def _dot(a, b):
    return jnp.dot(a, b, preferred_element_type=F32)


def _gelu(v):
    return 0.5 * v * (1.0 + jnp.tanh(0.7978845608028654 * (v + 0.044715 * (v * v * v))))


def front_kernel(
    bases_ref, embed_ref, convw_ref, convb_ref, wt_ref, cot_ref,
    grad_ref, aown_ref, sown_ref,
    bsend, ball, wcat, wc, wcp, oh, yb, st, xt, wt, qt, kv, ks, at, an, ath, aown, sbuf, sown, cotr,
    ss_b, rs_b, ss_w, rs_w, ss1, rs1, ss2, rs2, ss_c, rs_c, ss_k, rs_k, ss_s, rs_s, ss_t, rs_t, ss_a, rs_a,
    ss_d, rs_d,
):
    me = lax.axis_index("ctx")
    core = lax.rem(me, 2)
    x = lax.rem(me // 2, 4)
    y = me // 8
    chip = me // 2
    sib = me + 1 - 2 * core

    def ctx(yy, xx, cc):
        return (yy * 4 + lax.rem(xx, 4)) * 2 + cc

    def rcopy(src, dst, ssem, rsem, to):
        return pltpu.make_async_remote_copy(
            src_ref=src, dst_ref=dst, send_sem=ssem, recv_sem=rsem,
            device_id={"ctx": to}, device_id_type=MESH,
        )

    barrier = pltpu.get_barrier_semaphore()
    for d in range(1, 16):
        pl.semaphore_signal(barrier, inc=1, device_id={"ctx": lax.rem(me + d, 16)}, device_id_type=MESH)
    mine = bases_ref[...].astype(F32).astype(BF)
    bsend[...] = mine
    ball[pl.ds(_al(me * 80, 16), 80), :] = mine
    pl.semaphore_wait(barrier, 15)

    def bcopy(d):
        return rcopy(bsend, ball.at[pl.ds(_al(me * 80, 16), 80)], ss_b.at[d - 1], rs_b.at[d - 1], lax.rem(me + d, 16))

    def start_b(d, c):
        bcopy(d).start()
        return c

    lax.fori_loop(1, 16, start_b, 0)
    wcopy = rcopy(wt_ref, wt.at[pl.ds(_al(core * 192, 16), 192)], ss_w, rs_w, sib)
    wcopy.start()
    wt[pl.ds(_al(core * 192, 16), 192), :] = wt_ref[...]

    def fill(i, c):
        rows = pl.ds(_al(i * 256, 256), 256)
        for j in range(5):
            wcat[rows, 128 * j : 128 * j + 128] = jnp.zeros((256, 128), BF)
            wcat[rows, 128 * j : 128 * j + 96] = convw_ref[j, rows, :]
        r = lax.broadcasted_iota(jnp.int32, (256, 128), 0) + i * 256
        cc = lax.broadcasted_iota(jnp.int32, (256, 128), 1)
        pick = jnp.where(jnp.logical_and(r == cc + 96 * me, cc < 96), 1.0, 0.0)
        wcat[rows, 640:768] = pick.astype(BF)
        return c

    lax.fori_loop(0, 6, fill, 0)

    def comp(i, c):
        cols = pl.ds(_al(i * 256, 256), 256)
        prod = _dot(embed_ref[...], wcat[:, cols])
        wc[2 * i] = prod[:, 0:128]
        wc[2 * i + 1] = prod[:, 128:256]
        return c

    lax.fori_loop(0, 3, comp, 0)
    for b in range(4):
        for j in range(6):
            wcp[128 * b : 128 * b + 128, 128 * j : 128 * j + 128] = wc[j, pl.ds(b, 128, stride=4), :].astype(BF)
    yb[0:8, :] = jnp.zeros((8, 768), F32)
    yb[1288:1296, :] = jnp.zeros((8, 768), F32)

    def wait_b(d, c):
        bcopy(d).wait_recv()
        return c

    lax.fori_loop(1, 16, wait_b, 0)

    def taps(i, c):
        rows = pl.ds(_al(i * 256, 256), 256)
        bb = ball[rows, :].astype(F32)
        for b in range(4):
            oh[:, 128 * b : 128 * b + 128] = jnp.where(bb == float(b), 1.0, 0.0).astype(BF)
        yb[pl.ds(_al(i * 256 + 8, 8), 256), :] = _dot(oh[...], wcp[...])
        return c

    lax.fori_loop(0, 5, taps, 0)

    def act(q, c):
        win = pl.ds(_al(q * 128, 8), 144)
        pre = jnp.zeros((128, 128), F32) + convb_ref[...]
        for j in range(5):
            pre = pre + yb[win, 128 * j : 128 * j + 128][6 + j : 134 + j]
        val = yb[pl.ds(_al(q * 128 + 8, 8), 128), 640:768] + _gelu(pre)
        st[q // 5, :, pl.ds(_al(lax.rem(q, 5) * 128, 128), 128)] = val.T[0:96, :].astype(BF)
        return c

    own_rows = pl.ds(_al(me * 96, 16), 96)
    sends = []

    def s1(rel, ct):
        to = ctx(y, x + rel + 1, ct) if rel < 3 else ctx(1 - y, x, ct)
        return rcopy(st.at[ct], xt.at[own_rows], ss1.at[rel * 2 + ct], rs1.at[rel * 2 + core], to)

    for half in range(2):
        lax.fori_loop(5 * half, 5 * half + 5, act, 0)
        for rel in (3, 0, 2, 1):
            cp = s1(rel, half)
            cp.start()
            sends.append(cp)

        @pl.when(core == half)
        def _():
            xt[own_rows, :] = st[half]

        @pl.when(core != half)
        def _():
            rcopy(st.at[half], xt.at[own_rows], ss1.at[8], rs1.at[8], sib).start()

    def chip_rows(kk):
        return pl.ds(_al(kk * 192, 16), 192)

    def s1_wait(rel):
        for cs in range(2):
            rcopy(st.at[0], xt.at[own_rows], ss1.at[rel * 2 + cs], rs1.at[rel * 2 + cs], sib).wait_recv()

    s1_wait(3)
    ky = (1 - y) * 4 + x
    for d in (1, 3, 2):
        src = xt.at[chip_rows(ky), LA:640]
        cp = rcopy(src, src, ss2.at[2 + d], rs2.at[2 + d], ctx(y, x + d, core))
        cp.start()
        sends.append(cp)
    for d in (1, 3, 2):
        s1_wait(d - 1)
        src = xt.at[chip_rows(y * 4 + lax.rem(x + 4 - d, 4)), 0:LA]
        cp = rcopy(src, src, ss2.at[d - 1], rs2.at[d - 1], ctx(1 - y, x, core))
        cp.start()
        sends.append(cp)

    my_tok = pl.ds(_al(lax.rem(me, 8) * 80, 16), 80)
    cots = []
    for d in (1, 3, 2):
        for cc in range(2):
            cols = slice(768 * cc, 768 * cc + 768)
            cp = rcopy(cot_ref.at[:, cols], cotr.at[my_tok, cols], ss_c.at[2 * d - 2 + cc], rs_c.at[2 * d - 2 + core],
                       ctx(y, x + d, cc))
            cp.start()
            cots.append(cp)
    for cc in range(2):
        cols = slice(768 * cc, 768 * cc + 768)

        @pl.when(core == cc)
        def _():
            cotr[my_tok, cols] = cot_ref[:, cols]

        @pl.when(core != cc)
        def _():
            rcopy(cot_ref.at[:, cols], cotr.at[my_tok, cols], ss_c.at[6], rs_c.at[6], sib).start()

    wcopy.wait()
    rcopy(st.at[0], xt.at[own_rows], ss1.at[8], rs1.at[8], sib).wait_recv()
    for d in (1, 3, 2):
        src = xt.at[chip_rows(0), LA:640]
        rcopy(src, src, ss2.at[2 + d], rs2.at[2 + d], sib).wait_recv()
        src = xt.at[chip_rows(0), 0:LA]
        rcopy(src, src, ss2.at[d - 1], rs2.at[d - 1], sib).wait_recv()

    def sq(i, acc):
        v = xt[pl.ds(_al(i * 128, 128), 128), :].astype(F32)
        return acc + jnp.sum((v * v).reshape(16, 8, 640), axis=0)

    total = lax.fori_loop(0, 12, sq, jnp.zeros((8, 640), F32))
    scale = lax.rsqrt(jnp.sum(total, axis=0, keepdims=True) * (1.0 / 1536.0) + 1e-06)
    for h in range(2):
        pr = _dot(wt[192 * h : 192 * h + 192, :], xt[...]) * scale
        qt[h] = (pr[0:64] * 0.125).astype(BF)
        kv[core, h] = pr[64:192].astype(BF)
    kcopy = rcopy(kv.at[core], kv.at[core], ss_k, rs_k, sib)
    kcopy.start()

    scopy = rcopy(sbuf.at[1 - core], sown, ss_s, rs_s, sib)

    @pl.when(core == y)
    def _():
        r = lax.broadcasted_iota(jnp.int32, (160, 640), 0) + 160 * x
        cidx = lax.broadcasted_iota(jnp.int32, (160, 640), 1)
        pick = jnp.where(r == cidx, 1.0, 0.0).astype(BF)
        for n in range(6):
            part = lax.dot_general(pick, xt[256 * n : 256 * n + 256, :], (((1,), (1,)), ((), ())),
                                   preferred_element_type=F32).astype(BF)
            sbuf[0, :, 256 * n : 256 * n + 256] = part[0:80]
            sbuf[1, :, 256 * n : 256 * n + 256] = part[80:160]
        sown[...] = sbuf[core]
        scopy.start()

    kcopy.wait()
    for h in range(2):
        for half in range(2):
            ks[h, 640 * half : 640 * half + 640, :] = kv[half, h, 0:64, :].astype(F32).T.astype(BF)

    def attend(i, c):
        lanes = pl.ds(_al(i * 128, 128), 128)
        outs = []
        for h in range(2):
            s = _dot(ks[h], qt[h, :, lanes])
            p = jnp.exp(s - jnp.max(s, axis=0, keepdims=True))
            den = jnp.sum(p, axis=0, keepdims=True)
            pb = p.astype(BF)
            o = _dot(kv[0, h, 64:128, :], pb[0:640]) + _dot(kv[1, h, 64:128, :], pb[640:1280])
            outs.append(o / den)
        both = jnp.concatenate(outs, axis=0)
        at[:, lanes] = both.astype(BF)
        an[lanes, :] = both.T.astype(BF)
        return c

    lax.fori_loop(0, 5, attend, 0)

    kx = core * 4 + x

    def tcopy(cc):
        return rcopy(at.at[64 * cc : 64 * cc + 64], ath.at[pl.ds(_al(y * 64, 16), 64)], ss_t.at[cc], rs_t.at[y],
                     kx * 2 + cc)

    for cc in range(2):
        @pl.when(kx * 2 + cc == me)
        def _():
            ath[pl.ds(_al(y * 64, 16), 64), :] = at[64 * cc : 64 * cc + 64, :]

        @pl.when(kx * 2 + cc != me)
        def _():
            tcopy(cc).start()

    def acopy(j):
        return rcopy(an.at[80 * j : 80 * j + 80], aown.at[:, pl.ds(_al(chip * 128, 128), 128)], ss_a.at[j], rs_a.at[chip],
                     8 * core + j)

    for j in range(8):
        @pl.when(8 * core + j == me)
        def _():
            aown[:, pl.ds(_al(chip * 128, 128), 128)] = an[80 * j : 80 * j + 80, :]

        @pl.when(8 * core + j != me)
        def _():
            acopy(j).start()

    for d in (1, 3, 2):
        for cs in range(2):
            rcopy(cot_ref.at[:, 0:768], cotr.at[my_tok, 0:768], ss_c.at[2 * d - 2 + cs], rs_c.at[2 * d - 2 + cs],
                  sib).wait_recv()
    rcopy(cot_ref.at[:, 0:768], cotr.at[my_tok, 0:768], ss_c.at[6], rs_c.at[6], sib).wait_recv()
    half_cols = cotr.at[:, pl.ds(_al(core * 768, 128), 768)]
    dcopy = rcopy(half_cols, half_cols, ss_d, rs_d, sib)
    dcopy.start()

    def t_wait(slot):
        rcopy(at.at[0:64], ath.at[0:64], ss_t.at[0], rs_t.at[slot], sib).wait_recv()

    t_wait(1 - y)

    @pl.when(core != y)
    def _():
        t_wait(y)

    dcopy.wait()
    for n in range(3):
        cols = slice(512 * n, 512 * n + 512)
        grad_ref[:, cols] = _dot(ath[...], cotr[:, cols]).astype(BF)

    for k in range(8):
        @pl.when(2 * k + y != me)
        def _():
            rcopy(an.at[0:80], aown.at[:, 0:128], ss_a.at[0], rs_a.at[k], sib).wait_recv()

    @pl.when(core != y)
    def _():
        scopy.wait_recv()

    aown_ref[...] = aown[...]
    sown_ref[...] = sown[...]

    @pl.when(core == y)
    def _():
        scopy.wait_send()

    def send_b(d, c):
        bcopy(d).wait_send()
        return c

    lax.fori_loop(1, 16, send_b, 0)
    for cp in sends + cots:
        cp.wait_send()
    rcopy(st.at[0], xt.at[own_rows], ss1.at[8], rs1.at[8], sib).wait_send()
    rcopy(cot_ref.at[:, 0:768], cotr.at[my_tok, 0:768], ss_c.at[6], rs_c.at[6], sib).wait_send()
    for cc in range(2):
        @pl.when(kx * 2 + cc != me)
        def _():
            tcopy(cc).wait_send()
    for j in range(8):
        @pl.when(8 * core + j != me)
        def _():
            acopy(j).wait_send()


def grad_kernel(g_ref, out_ref, yr, zs, zr, fb, rc, ss_y, rs_y, ss_z, rs_z, ss_f, rs_f):
    dp = lax.axis_index("dp")
    me = lax.axis_index("ctx")
    yh, z = dp // 16, lax.rem(dp, 16)
    yl, rest = me // 8, lax.rem(me, 8)
    ring = 2 * yh + yl

    def rcopy(src, dst, ssem, rsem, to):
        return pltpu.make_async_remote_copy(
            src_ref=src, dst_ref=dst, send_sem=ssem, recv_sem=rsem, device_id=to, device_id_type=MESH
        )

    def ring_dev(e):
        r = lax.rem(ring + e, 4)
        return (r // 2) * 16 + z, lax.rem(r, 2) * 8 + rest

    barrier = pltpu.get_barrier_semaphore()

    def sig(d, c):
        pl.semaphore_signal(barrier, inc=1, device_id=(lax.rem(dp + d, 32), me), device_id_type=MESH)
        return c

    lax.fori_loop(1, 32, sig, 0)
    for e in (1, 3):
        pl.semaphore_signal(barrier, inc=1, device_id=ring_dev(e), device_id_type=MESH)
    pl.semaphore_wait(barrier, 33)

    def block(r):
        return pl.ds(_al(lax.rem(r, 2) * 64, 16), 64), pl.ds(_al((r // 2) * 768, 128), 768)

    ysend = []
    for e in (1, 2, 3):
        rows, cols = block(lax.rem(ring + e, 4))
        cp = rcopy(g_ref.at[rows, cols], yr.at[e - 1], ss_y.at[e - 1], rs_y.at[e - 1], ring_dev(e))
        cp.start()
        ysend.append(cp)
    rows, cols = block(ring)
    acc = g_ref[rows, cols].astype(F32)
    for e in (1, 3, 2):
        ysend[e - 1].wait_recv()
        acc = acc + yr[e - 1].astype(F32)
    zs[...] = acc.astype(BF)

    def zcopy(q):
        return rcopy(zs.at[16 * (q // 3) : 16 * (q // 3) + 16, 256 * (q % 3) : 256 * (q % 3) + 256], zr.at[z],
                     ss_z.at[q], rs_z.at[z], (yh * 16 + q, me))

    for q in range(12):
        @pl.when(z != q)
        def _():
            zcopy(q).start()

    zrows = pl.ds(_al((z // 3) * 16, 16), 16)
    zlane = lax.rem(z, 3) * 256

    def fcopy(d):
        return rcopy(rc, fb.at[zrows, pl.ds(_al(yh * 768 + zlane, 128), 256)], ss_f.at[d - 1], rs_f.at[yh * 12 + z],
                     (lax.rem(dp + d, 32), me))

    @pl.when(z < 12)
    def _():
        zr[z] = zs[zrows, pl.ds(_al(zlane, 128), 256)]

        def wait_z(s, c):
            @pl.when(s != z)
            def _():
                rcopy(rc, zr.at[s], ss_z.at[0], rs_z.at[s], (yh * 16 + s, me)).wait_recv()
            return c

        lax.fori_loop(0, 16, wait_z, 0)
        tot = zr[0].astype(F32)
        for s in range(1, 16):
            tot = tot + zr[s].astype(F32)
        rc[...] = tot.astype(BF)
        fb[zrows, pl.ds(_al(yh * 768 + zlane, 128), 256)] = tot.astype(BF)

        def start_f(d, c):
            fcopy(d).start()
            return c

        lax.fori_loop(1, 32, start_f, 0)

    def wait_f(s, c):
        @pl.when(s != yh * 12 + z + jnp.where(z < 12, 0, 1000))
        def _():
            rcopy(rc, fb.at[0:16, 0:256], ss_f.at[0], rs_f.at[s], (dp, me)).wait_recv()
        return c

    lax.fori_loop(0, 24, wait_f, 0)
    out_ref[...] = fb[...]
    for cp in ysend:
        cp.wait_send()
    for q in range(12):
        @pl.when(z != q)
        def _():
            zcopy(q).wait_send()

    @pl.when(z < 12)
    def _():
        def wait_s(d, c):
            fcopy(d).wait_send()
            return c

        lax.fori_loop(1, 32, wait_s, 0)


def per_device(bases, embed_w, conv_w, conv_b, norm_g, qkv_w, wo, cotangent):
    vm = pl.BlockSpec(memory_space=pltpu.VMEM)
    dma = pltpu.SemaphoreType.DMA
    wo_all = lax.all_gather(wo, "ctx", axis=0, tiled=True)
    wt = (qkv_w.T.astype(F32) * norm_g[None, :]).astype(BF)
    bias = jnp.pad(conv_b, (0, 32))[None]
    V = pltpu.VMEM
    grad, aown, sown = pl.pallas_call(
        front_kernel,
        out_shape=(
            jax.ShapeDtypeStruct((128, 1536), BF),
            jax.ShapeDtypeStruct((80, 1024), BF),
            jax.ShapeDtypeStruct((80, 1536), BF),
        ),
        in_specs=[vm] * 6,
        out_specs=(vm,) * 3,
        scratch_shapes=[
            V((80, 128), BF), V((1280, 128), BF), V((1536, 768), BF), V((6, 512, 128), F32), V((512, 768), BF),
            V((256, 512), BF), V((1296, 768), F32), V((2, 96, 640), BF), V((1536, 640), BF), V((384, 1536), BF),
            V((2, 64, 640), BF), V((2, 2, 128, 640), BF), V((2, 1280, 64), BF), V((128, 640), BF), V((640, 128), BF),
            V((128, 640), BF), V((80, 1024), BF), V((2, 80, 1536), BF), V((80, 1536), BF), V((640, 1536), BF),
            dma((15,)), dma((15,)), dma, dma, dma((9,)), dma((9,)), dma((6,)), dma((6,)), dma((7,)), dma((7,)),
            dma, dma, dma, dma, dma((2,)), dma((2,)), dma((8,)), dma((8,)), dma, dma,
        ],
        compiler_params=pltpu.CompilerParams(collective_id=0, has_side_effects=True, vmem_limit_bytes=56 << 20),
        name="front",
    )(bases.reshape(80, 128), embed_w, conv_w, bias, wt, cotangent[0])
    wo_grad = pl.pallas_call(
        grad_kernel,
        out_shape=jax.ShapeDtypeStruct((64, 1536), BF),
        in_specs=[vm],
        out_specs=vm,
        scratch_shapes=[
            V((3, 64, 768), BF), V((64, 768), BF), V((16, 16, 256), BF), V((64, 1536), BF), V((16, 256), BF),
            dma((3,)), dma((3,)), dma((12,)), dma((16,)), dma((31,)), dma((24,)),
        ],
        compiler_params=pltpu.CompilerParams(collective_id=1, has_side_effects=True, vmem_limit_bytes=20 << 20),
        name="gradsum",
    )(grad)
    layer_out = (sown.astype(F32) + _dot(aown, wo_all)).astype(BF)[None]
    return layer_out, wo_grad


def solution(mesh):
    return jax.shard_map(
        per_device,
        mesh=mesh,
        in_specs=(
            P("dp", "ctx"), P(), P(None, None, "ctx"), P("ctx"), P(), P(None, "ctx"), P("ctx", None),
            P("dp", "ctx", None),
        ),
        out_specs=(P("dp", "ctx", None), P("ctx", None)),
        check_vma=False,
    )
```

```python
import functools

import jax
import jax.numpy as jnp
from jax import lax
from jax.experimental import pallas as pl
from jax.experimental.pallas import tpu as pltpu
from jax.sharding import PartitionSpec as P

MESH = pl.DeviceIdType.MESH
BF = jnp.bfloat16
F32 = jnp.float32
LA = 384


def _al(v, m):
    return pl.multiple_of(v, m)


def _dot(a, b):
    return jnp.dot(a, b, preferred_element_type=F32)


def _gelu(v):
    return 0.5 * v * (1.0 + jnp.tanh(0.7978845608028654 * (v + 0.044715 * (v * v * v))))


def layer_kernel(
    bases_ref, embed_ref, convt_ref, convb_ref, qkvt_ref, gain_ref, wo_ref, cot_ref,
    out_ref, grad_ref,
    bsend, ball, wcat, wc, wcp, oh, yb, st, xt, wt, qt, kv, ks, sc, at, an, ath, aown, sbuf, sown, cotr, wof,
    gl, yr, zs, nr, fr, rc, fb,
    ss_b, rs_b, ss_w, rs_w, ss1, rs1, ss2, rs2, ss_c, rs_c, ss_k, rs_k, ss_s, rs_s, ss_t, rs_t, ss_a, rs_a,
    ss_d, rs_d, ss_o, rs_o, ss_p, rs_p, ss_q, rs_q, ss_y, rs_y, ss_n, rs_n, ss_f, rs_f, ss_g, rs_g,
):
    dp = lax.axis_index("dp")
    me = lax.axis_index("ctx")
    yh, z = dp // 16, lax.rem(dp, 16)
    za, zb = z // 4, lax.rem(z, 4)
    core = lax.rem(me, 2)
    chip = me // 2
    x = lax.rem(chip, 4)
    y = me // 8
    sib = me + 1 - 2 * core
    ring = 2 * yh + y

    def ctx(yy, xx, cc):
        return (yy * 4 + lax.rem(xx, 4)) * 2 + cc

    def rcopy(src, dst, ssem, rsem, to):
        return pltpu.make_async_remote_copy(
            src_ref=src, dst_ref=dst, send_sem=ssem, recv_sem=rsem,
            device_id=to if isinstance(to, tuple) else (dp, to), device_id_type=MESH,
        )

    def ring_dev(e):
        r = lax.rem(ring + e, 4)
        return (r // 2) * 16 + z, lax.rem(r, 2) * 8 + lax.rem(me, 8)

    def near(e):
        return yh * 16 + za * 4 + lax.rem(zb + e, 4), me

    def across(e):
        return (1 - yh) * 16 + za * 4 + lax.rem(zb + e, 4), me

    def far(e):
        return yh * 16 + lax.rem(za + e, 4) * 4 + zb, me

    barrier = pltpu.get_barrier_semaphore()
    greet = [(dp, lax.rem(me + d, 16)) for d in range(1, 16)]
    greet += [near(e) for e in (1, 2, 3)] + [far(e) for e in (1, 2, 3)] + [across(e) for e in range(4)]
    greet += [((1 - yh) * 16 + z, (1 - y) * 8 + lax.rem(me, 8))]
    for to in greet:
        pl.semaphore_signal(barrier, inc=1, device_id=to, device_id_type=MESH)
    mine = bases_ref[...].astype(F32).astype(BF)
    bsend[...] = mine
    ball[pl.ds(_al(me * 80, 16), 80), :] = mine
    wrows = pl.ds(_al(core * 192, 16), 192)
    wt[wrows, :] = (qkvt_ref[...].astype(F32) * gain_ref[...]).astype(BF)
    pl.semaphore_wait(barrier, len(greet))

    def bcopy(d):
        return rcopy(bsend, ball.at[pl.ds(_al(me * 80, 16), 80)], ss_b.at[d - 1], rs_b.at[d - 1], lax.rem(me + d, 16))

    def start_b(d, c):
        bcopy(d).start()
        return c

    lax.fori_loop(1, 16, start_b, 0)
    wcopy = rcopy(wt.at[wrows], wt.at[wrows], ss_w, rs_w, sib)
    wcopy.start()
    sends = []

    wo_rows = pl.ds(_al(me * 64, 16), 64)
    for d in (1, 3, 2):
        for cc in range(2):
            cols = slice(768 * cc, 768 * cc + 768)
            cp = rcopy(wo_ref.at[:, cols], wof.at[wo_rows, cols], ss_o.at[2 * d - 2 + cc], rs_o.at[2 * d - 2 + core],
                       ctx(y, x + d, cc))
            cp.start()
            sends.append(cp)
    for cc in range(2):
        cols = slice(768 * cc, 768 * cc + 768)

        @pl.when(core == cc)
        def _():
            wof[wo_rows, cols] = wo_ref[:, cols]

        @pl.when(core != cc)
        def _():
            rcopy(wo_ref.at[:, cols], wof.at[wo_rows, cols], ss_o.at[6], rs_o.at[6], sib).start()

    for j in range(6):
        wcat[128 * j + 96 : 128 * j + 128, :] = jnp.zeros((32, 1536), BF)
    for j in range(5):
        wcat[128 * j : 128 * j + 96, :] = convt_ref[96 * j : 96 * j + 96, :]
    r = lax.broadcasted_iota(jnp.int32, (96, 1536), 0) + 96 * me
    cc = lax.broadcasted_iota(jnp.int32, (96, 1536), 1)
    wcat[640:736, :] = jnp.where(r == cc, 1.0, 0.0).astype(BF)

    def comp(i, c):
        prod = lax.dot_general(embed_ref[...], wcat[pl.ds(_al(i * 256, 256), 256), :], (((1,), (1,)), ((), ())),
                               preferred_element_type=F32)
        wc[2 * i] = prod[:, 0:128]
        wc[2 * i + 1] = prod[:, 128:256]
        return c

    lax.fori_loop(0, 3, comp, 0)
    for b in range(4):
        for j in range(6):
            wcp[128 * b : 128 * b + 128, 128 * j : 128 * j + 128] = wc[j, pl.ds(b, 128, stride=4), :].astype(BF)
    yb[0:8, :] = jnp.zeros((8, 768), F32)
    yb[1288:1296, :] = jnp.zeros((8, 768), F32)

    def wait_b(d, c):
        bcopy(d).wait_recv()
        return c

    lax.fori_loop(1, 16, wait_b, 0)

    def taps(i, c):
        rows = pl.ds(_al(i * 256, 256), 256)
        bb = ball[rows, :].astype(F32)
        for b in range(4):
            oh[:, 128 * b : 128 * b + 128] = jnp.where(bb == float(b), 1.0, 0.0).astype(BF)
        yb[pl.ds(_al(i * 256 + 8, 8), 256), :] = _dot(oh[...], wcp[...])
        return c

    lax.fori_loop(0, 5, taps, 0)

    bias = convb_ref[...]

    def act(q, c):
        win = pl.ds(_al(q * 128, 8), 144)
        pre = jnp.zeros((128, 128), F32)
        for j in range(5):
            pre = pre + yb[win, 128 * j : 128 * j + 128][6 + j : 134 + j]
        own = yb[pl.ds(_al(q * 128 + 8, 8), 128), 640:768]
        val = own.T[0:96] + _gelu(pre.T[0:96] + bias)
        st[q // 5, :, pl.ds(_al(lax.rem(q, 5) * 128, 128), 128)] = val.astype(BF)
        return c

    own_rows = pl.ds(_al(me * 96, 16), 96)

    def s1(rel, ct):
        to = ctx(y, x + rel + 1, ct) if rel < 3 else ctx(1 - y, x, ct)
        return rcopy(st.at[ct], xt.at[own_rows], ss1.at[rel * 2 + ct], rs1.at[rel * 2 + core], to)

    for half in range(2):
        lax.fori_loop(5 * half, 5 * half + 5, act, 0)
        for rel in (3, 0, 2, 1):
            cp = s1(rel, half)
            cp.start()
            sends.append(cp)

        @pl.when(core == half)
        def _():
            xt[own_rows, :] = st[half]

        @pl.when(core != half)
        def _():
            rcopy(st.at[half], xt.at[own_rows], ss1.at[8], rs1.at[8], sib).start()

    def chip_rows(kk):
        return pl.ds(_al(kk * 192, 16), 192)

    def s1_wait(rel):
        for cs in range(2):
            rcopy(st.at[0], xt.at[own_rows], ss1.at[rel * 2 + cs], rs1.at[rel * 2 + cs], sib).wait_recv()

    s1_wait(3)
    ky = (1 - y) * 4 + x
    for d in (1, 3, 2):
        src = xt.at[chip_rows(ky), LA:640]
        cp = rcopy(src, src, ss2.at[2 + d], rs2.at[2 + d], ctx(y, x + d, core))
        cp.start()
        sends.append(cp)
    for d in (1, 3, 2):
        s1_wait(d - 1)
        src = xt.at[chip_rows(y * 4 + lax.rem(x + 4 - d, 4)), 0:LA]
        cp = rcopy(src, src, ss2.at[d - 1], rs2.at[d - 1], ctx(1 - y, x, core))
        cp.start()
        sends.append(cp)

    my_tok = pl.ds(_al(lax.rem(me, 8) * 80, 16), 80)
    cots = []
    for d in (1, 3, 2):
        for cc in range(2):
            cols = slice(768 * cc, 768 * cc + 768)
            cp = rcopy(cot_ref.at[:, cols], cotr.at[my_tok, cols], ss_c.at[2 * d - 2 + cc], rs_c.at[2 * d - 2 + core],
                       ctx(y, x + d, cc))
            cp.start()
            cots.append(cp)
    for cc in range(2):
        cols = slice(768 * cc, 768 * cc + 768)

        @pl.when(core == cc)
        def _():
            cotr[my_tok, cols] = cot_ref[:, cols]

        @pl.when(core != cc)
        def _():
            rcopy(cot_ref.at[:, cols], cotr.at[my_tok, cols], ss_c.at[6], rs_c.at[6], sib).start()

    def o_wait(slot):
        rcopy(wo_ref.at[:, 0:768], wof.at[0:64, 0:768], ss_o.at[0], rs_o.at[slot], sib).wait_recv()

    wo_cols = pl.ds(_al(core * 768, 128), 768)
    for slot in (0, 1, 4, 5, 2, 3, 6):
        o_wait(slot)
    for i, e in enumerate((1, 3)):
        part = wof.at[pl.ds(_al(y * 512 + 256 * i, 16), 256), wo_cols]
        cp = rcopy(part, part, ss_p.at[i], rs_p.at[i], ring_dev(e))
        cp.start()
        sends.append(cp)

    wcopy.wait()
    rcopy(st.at[0], xt.at[own_rows], ss1.at[8], rs1.at[8], sib).wait_recv()
    for d in (1, 3, 2):
        src = xt.at[chip_rows(0), LA:640]
        rcopy(src, src, ss2.at[2 + d], rs2.at[2 + d], sib).wait_recv()
        src = xt.at[chip_rows(0), 0:LA]
        rcopy(src, src, ss2.at[d - 1], rs2.at[d - 1], sib).wait_recv()

    def sq(i, acc):
        v = xt[pl.ds(_al(i * 128, 128), 128), :].astype(F32)
        return acc + jnp.sum((v * v).reshape(16, 8, 640), axis=0)

    total = lax.fori_loop(0, 12, sq, jnp.zeros((8, 640), F32))
    scale = lax.rsqrt(jnp.sum(total, axis=0, keepdims=True) * (1.0 / 1536.0) + 1e-06)
    for h in range(2):
        pr = _dot(wt[192 * h : 192 * h + 192, :], xt[...]) * scale
        qt[h] = (pr[0:64] * 0.125).astype(BF)
        kv[core, h] = pr[64:192].astype(BF)
    kcopy = rcopy(kv.at[core], kv.at[core], ss_k, rs_k, sib)
    kcopy.start()

    scopy = rcopy(sbuf.at[1 - core], sown, ss_s, rs_s, sib)

    @pl.when(core == y)
    def _():
        r = lax.broadcasted_iota(jnp.int32, (160, 640), 0) + 160 * x
        cidx = lax.broadcasted_iota(jnp.int32, (160, 640), 1)
        pick = jnp.where(r == cidx, 1.0, 0.0).astype(BF)
        for n in range(6):
            part = lax.dot_general(pick, xt[256 * n : 256 * n + 256, :], (((1,), (1,)), ((), ())),
                                   preferred_element_type=F32).astype(BF)
            sbuf[0, :, 256 * n : 256 * n + 256] = part[0:80]
            sbuf[1, :, 256 * n : 256 * n + 256] = part[80:160]
        sown[...] = sbuf[core]
        scopy.start()

    kcopy.wait()
    for h in range(2):
        for half in range(2):
            ks[h, 640 * half : 640 * half + 640, :] = kv[half, h, 0:64, :].astype(F32).T.astype(BF)

    steps = [(h, a, w) for a, w in ((0, 256), (256, 256), (512, 128)) for h in range(2)]

    def score(n):
        h, a, w = steps[n]
        sc[n % 2, :, 0:w] = _dot(ks[h], qt[h, :, a : a + w])

    score(0)
    outs = [None, None]
    for n, (h, a, w) in enumerate(steps):
        if n + 1 < len(steps):
            score(n + 1)
        s = sc[n % 2, :, 0:w]
        p = jnp.exp(s - jnp.max(s, axis=0, keepdims=True))
        den = jnp.sum(p, axis=0, keepdims=True)
        pb = p.astype(BF)
        o = (_dot(kv[0, h, 64:128, :], pb[0:640]) + _dot(kv[1, h, 64:128, :], pb[640:1280])) / den
        at[64 * h : 64 * h + 64, a : a + w] = o.astype(BF)
        outs[h] = o
        if h == 1:
            an[a : a + w, :] = jnp.concatenate(outs, axis=0).T.astype(BF)

    kx = core * 4 + x

    def tcopy(cc):
        return rcopy(at.at[64 * cc : 64 * cc + 64], ath.at[pl.ds(_al(y * 64, 16), 64)], ss_t.at[cc], rs_t.at[y],
                     kx * 2 + cc)

    for cc in range(2):
        @pl.when(kx * 2 + cc == me)
        def _():
            ath[pl.ds(_al(y * 64, 16), 64), :] = at[64 * cc : 64 * cc + 64, :]

        @pl.when(kx * 2 + cc != me)
        def _():
            tcopy(cc).start()

    def acopy(j):
        return rcopy(an.at[80 * j : 80 * j + 80], aown.at[:, pl.ds(_al(chip * 128, 128), 128)], ss_a.at[j], rs_a.at[chip],
                     8 * core + j)

    for j in range(8):
        @pl.when(8 * core + j == me)
        def _():
            aown[:, pl.ds(_al(chip * 128, 128), 128)] = an[80 * j : 80 * j + 80, :]

        @pl.when(8 * core + j != me)
        def _():
            acopy(j).start()

    for i in range(2):
        part = wof.at[0:256, wo_cols]
        rcopy(part, part, ss_p.at[i], rs_p.at[i], sib).wait_recv()
    ocopy = rcopy(wof.at[:, wo_cols], wof.at[:, wo_cols], ss_q, rs_q, sib)

    for d in (1, 3, 2):
        for cs in range(2):
            rcopy(cot_ref.at[:, 0:768], cotr.at[my_tok, 0:768], ss_c.at[2 * d - 2 + cs], rs_c.at[2 * d - 2 + cs],
                  sib).wait_recv()
    rcopy(cot_ref.at[:, 0:768], cotr.at[my_tok, 0:768], ss_c.at[6], rs_c.at[6], sib).wait_recv()
    half_cols = cotr.at[:, pl.ds(_al(core * 768, 128), 768)]
    dcopy = rcopy(half_cols, half_cols, ss_d, rs_d, sib)
    dcopy.start()
    ocopy.start()

    def t_wait(slot):
        rcopy(at.at[0:64], ath.at[0:64], ss_t.at[0], rs_t.at[slot], sib).wait_recv()

    t_wait(1 - y)

    @pl.when(core != y)
    def _():
        t_wait(y)

    dcopy.wait()
    for n in range(3):
        cols = slice(512 * n, 512 * n + 512)
        gl[:, cols] = _dot(ath[...], cotr[:, cols]).astype(BF)

    def block(r):
        return pl.ds(_al(lax.rem(r, 2) * 64, 16), 64), pl.ds(_al((r // 2) * 768, 128), 768)

    ysend = []
    for e in (1, 3, 2):
        rows, cols = block(lax.rem(ring + e, 4))
        cp = rcopy(gl.at[rows, cols], yr.at[e - 1], ss_y.at[e - 1], rs_y.at[e - 1], ring_dev(e))
        cp.start()
        ysend.append(cp)

    for k in range(8):
        @pl.when(2 * k + y != me)
        def _():
            rcopy(an.at[0:80], aown.at[:, 0:128], ss_a.at[0], rs_a.at[k], sib).wait_recv()

    @pl.when(core != y)
    def _():
        scopy.wait_recv()

    ocopy.wait()
    for n in range(6):
        cols = slice(256 * n, 256 * n + 256)
        out_ref[:, cols] = (sown[:, cols].astype(F32) + _dot(aown[...], wof[:, cols])).astype(BF)

    rows, cols = block(ring)
    acc = gl[rows, cols].astype(F32)
    for e, cp in zip((1, 3, 2), ysend):
        cp.wait_recv()
        acc = acc + yr[e - 1].astype(F32)
    zs[...] = acc.astype(BF)

    late = list(ysend)
    nsend = []
    for e in (1, 3, 2):
        cp = rcopy(zs.at[pl.ds(_al(lax.rem(zb + e, 4) * 16, 16), 16)], nr.at[e - 1], ss_n.at[e - 1], rs_n.at[e - 1], near(e))
        cp.start()
        nsend.append(cp)
    zrows = pl.ds(_al(zb * 16, 16), 16)
    acc = zs[zrows, :].astype(F32)
    for e, cp in zip((1, 3, 2), nsend):
        cp.wait_recv()
        acc = acc + nr[e - 1].astype(F32)
    fr[za] = acc.astype(BF)
    fsend = []
    for e in (2, 1, 3):
        cp = rcopy(fr.at[za], fr.at[za], ss_f.at[e - 1], rs_f.at[e - 1], far(e))
        cp.start()
        fsend.append(cp)
    for cp in fsend:
        cp.wait_recv()
    acc = fr[0].astype(F32)
    for s in range(1, 4):
        acc = acc + fr[s].astype(F32)
    rc[...] = acc.astype(BF)
    fcols = pl.ds(_al(yh * 768, 128), 768)
    fb[zrows, fcols] = rc[...]
    gsend = []
    for i, to in enumerate([across(e) for e in range(4)] + [near(e) for e in (1, 2, 3)]):
        cp = rcopy(rc, fb.at[zrows, fcols], ss_g.at[i], rs_g.at[i], to)
        cp.start()
        gsend.append(cp)
    for cp in gsend:
        cp.wait_recv()
    grad_ref[...] = fb[...]

    @pl.when(core == y)
    def _():
        scopy.wait_send()

    def send_b(d, c):
        bcopy(d).wait_send()
        return c

    lax.fori_loop(1, 16, send_b, 0)
    for cp in sends + cots + late + nsend + fsend + gsend:
        cp.wait_send()
    rcopy(st.at[0], xt.at[own_rows], ss1.at[8], rs1.at[8], sib).wait_send()
    rcopy(cot_ref.at[:, 0:768], cotr.at[my_tok, 0:768], ss_c.at[6], rs_c.at[6], sib).wait_send()
    rcopy(wo_ref.at[:, 0:768], wof.at[wo_rows, 0:768], ss_o.at[6], rs_o.at[6], sib).wait_send()
    for cc in range(2):
        @pl.when(kx * 2 + cc != me)
        def _():
            tcopy(cc).wait_send()
    for j in range(8):
        @pl.when(8 * core + j != me)
        def _():
            acopy(j).wait_send()


def per_device(bases, embed_w, conv_w, conv_b, norm_g, qkv_w, wo, cotangent):
    vm = pl.BlockSpec(memory_space=pltpu.VMEM)
    V = pltpu.VMEM

    def sems(n):
        return [pltpu.SemaphoreType.DMA((n,)), pltpu.SemaphoreType.DMA((n,))]

    one = [pltpu.SemaphoreType.DMA, pltpu.SemaphoreType.DMA]
    out, wo_grad = pl.pallas_call(
        layer_kernel,
        out_shape=(jax.ShapeDtypeStruct((80, 1536), BF), jax.ShapeDtypeStruct((64, 1536), BF)),
        in_specs=[vm] * 8,
        out_specs=(vm,) * 2,
        scratch_shapes=[
            V((80, 128), BF), V((1280, 128), BF), V((768, 1536), BF), V((6, 512, 128), F32), V((512, 768), BF),
            V((256, 512), BF), V((1296, 768), F32), V((2, 96, 640), BF), V((1536, 640), BF), V((384, 1536), BF),
            V((2, 64, 640), BF), V((2, 2, 128, 640), BF), V((2, 1280, 64), BF), V((2, 1280, 256), F32),
            V((128, 640), BF), V((640, 128), BF), V((128, 640), BF), V((80, 1024), BF), V((2, 80, 1536), BF),
            V((80, 1536), BF), V((640, 1536), BF), V((1024, 1536), BF),
            V((128, 1536), BF), V((3, 64, 768), BF), V((64, 768), BF), V((3, 16, 768), BF), V((4, 16, 768), BF),
            V((16, 768), BF), V((64, 1536), BF),
        ] + sems(15) + one + sems(9) + sems(6) + sems(7) + one + one + sems(2) + sems(8) + one + sems(7) + sems(2) + one
        + sems(3) + sems(3) + sems(3) + sems(7),
        compiler_params=pltpu.CompilerParams(collective_id=0, has_side_effects=True, vmem_limit_bytes=56 << 20),
        name="layer",
    )(bases.reshape(80, 128), embed_w, conv_w.transpose(0, 2, 1).reshape(480, 1536), conv_b.reshape(96, 1), qkv_w.T,
      norm_g[None], wo, cotangent[0])
    return out[None], wo_grad


def solution(mesh):
    return jax.shard_map(
        per_device,
        mesh=mesh,
        in_specs=(
            P("dp", "ctx"), P(), P(None, None, "ctx"), P("ctx"), P(), P(None, "ctx"), P("ctx", None),
            P("dp", "ctx", None),
        ),
        out_specs=(P("dp", "ctx", None), P("ctx", None)),
        check_vma=False,
    )
```

```python
import functools

import jax
import jax.numpy as jnp
from jax import lax
from jax.experimental import pallas as pl
from jax.experimental.pallas import tpu as pltpu
from jax.sharding import PartitionSpec as P

MESH = pl.DeviceIdType.MESH
BF = jnp.bfloat16
F32 = jnp.float32
LA = 384


def _al(v, m):
    return pl.multiple_of(v, m)


def _dot(a, b):
    return jnp.dot(a, b, preferred_element_type=F32)


def _gelu(v):
    return 0.5 * v * (1.0 + jnp.tanh(0.7978845608028654 * (v + 0.044715 * (v * v * v))))


def layer_kernel(
    bases_hbm, embed_hbm, convt_hbm, convb_hbm, qkvt_hbm, gain_hbm, wo_hbm, cot_hbm,
    out_ref, grad_ref,
    ball, bsc, wcat, wc, wcp, oh, yb, st, xt, wt, qt, kv, ks, sc, at, an, ath, aown, sbuf, sown, cotr, wof,
    gl, yr, zs, nr, fr, rc, fb, acc, bases_ref, embed_ref, convb_ref, qkvt_ref, gain_ref, ld,
    ss_b, rs_b, ss_w, rs_w, ss1, rs1, ss2, rs2, ss_c, rs_c, ss_k, rs_k, ss_s, rs_s, ss_t, rs_t, ss_a, rs_a,
    ss_d, rs_d, ss_o, rs_o, ss_p, rs_p, ss_q, rs_q, ss_y, rs_y, ss_n, rs_n, ss_f, rs_f, ss_g, rs_g,
):
    dp = lax.axis_index("dp")
    me = lax.axis_index("ctx")
    yh, z = dp // 16, lax.rem(dp, 16)
    za, zb = z // 4, lax.rem(z, 4)
    core = lax.rem(me, 2)
    chip = me // 2
    x = lax.rem(chip, 4)
    y = me // 8
    sib = me + 1 - 2 * core
    ring = 2 * yh + y

    def ctx(yy, xx, cc):
        return (yy * 4 + lax.rem(xx, 4)) * 2 + cc

    def rcopy(src, dst, ssem, rsem, to):
        return pltpu.make_async_remote_copy(
            src_ref=src, dst_ref=dst, send_sem=ssem, recv_sem=rsem,
            device_id=to if isinstance(to, tuple) else (dp, to), device_id_type=MESH,
        )

    def ring_dev(e):
        r = lax.rem(ring + e, 4)
        return (r // 2) * 16 + z, lax.rem(r, 2) * 8 + lax.rem(me, 8)

    def near(e):
        return yh * 16 + za * 4 + lax.rem(zb + e, 4), me

    def across(e):
        return (1 - yh) * 16 + za * 4 + lax.rem(zb + e, 4), me

    def far(e):
        return yh * 16 + lax.rem(za + e, 4) * 4 + zb, me

    wo_rows = pl.ds(_al(me * 64, 16), 64)
    wo_other = pl.ds(_al((me + 8 - 16 * y) * 64, 16), 64)
    my_tok = pl.ds(_al(lax.rem(me, 8) * 80, 16), 80)
    barrier = pltpu.get_barrier_semaphore()
    greet = [(dp, lax.rem(me + d, 16)) for d in range(1, 16)]
    greet += [near(e) for e in (1, 2, 3)] + [far(e) for e in (1, 2, 3)] + [across(e) for e in range(4)]
    greet += [((1 - yh) * 16 + z, (1 - y) * 8 + lax.rem(me, 8))]
    for to in greet:
        pl.semaphore_signal(barrier, inc=1, device_id=to, device_id_type=MESH)
    loads = [
        pltpu.make_async_copy(src, dst, ld.at[i])
        for i, (src, dst) in enumerate(
            [(bases_hbm, bases_ref), (embed_hbm, embed_ref)]
            + [(convt_hbm.at[96 * j : 96 * j + 96], wcat.at[128 * j : 128 * j + 96]) for j in range(5)]
            + [(qkvt_hbm, qkvt_ref), (gain_hbm, gain_ref), (convb_hbm, convb_ref)]
            + [(wo_hbm, wof.at[wo_rows]), (cot_hbm, cotr.at[my_tok])]
        )
    ]
    for cp in loads:
        cp.start()
    loads[0].wait()
    ball[pl.ds(_al(me * 80, 16), 80), :] = bases_ref[...].astype(F32).astype(BF)
    pl.semaphore_wait(barrier, len(greet))

    plane = [(0, 1), (0, 3), (1, 0), (1, 1), (1, 3), (0, 2), (1, 2)]

    def ball_of(dev):
        return ball.at[pl.ds(_al(dev * 80, 16), 80)]

    def ysel(dy):
        return y + dy - 2 * dy * y

    bplane = []
    for i, (dy, dx) in enumerate(plane):
        cp = rcopy(ball_of(me), ball_of(me), ss_b.at[i], rs_b.at[i], ctx(ysel(dy), x + dx, core))
        cp.start()
        bplane.append(cp)
    bsib = [rcopy(ball_of(me), ball_of(me), ss_b.at[7], rs_b.at[7], sib)]
    bsib[0].start()

    for j in range(6):
        wcat[128 * j + 96 : 128 * j + 128, :] = jnp.zeros((32, 1536), BF)
    r = lax.broadcasted_iota(jnp.int32, (96, 1536), 0) + 96 * me
    cc = lax.broadcasted_iota(jnp.int32, (96, 1536), 1)
    wcat[640:736, :] = jnp.where(r == cc, 1.0, 0.0).astype(BF)
    for cp in loads[1:7]:
        cp.wait()

    def comp(i, c):
        prod = lax.dot_general(embed_ref[...], wcat[pl.ds(_al(i * 256, 256), 256), :], (((1,), (1,)), ((), ())),
                               preferred_element_type=F32)
        wc[2 * i] = prod[:, 0:128]
        wc[2 * i + 1] = prod[:, 128:256]
        return c

    lax.fori_loop(0, 2, comp, 0)
    for i, (dy, dx) in enumerate(plane):
        bplane[i].wait_recv()
        src = ball_of(ctx(ysel(dy), x + 4 - dx, core))
        cp = rcopy(src, src, ss_b.at[8 + i], rs_b.at[8 + i], sib)
        cp.start()
        bsib.append(cp)

    for cp in loads[7:12]:
        cp.wait()

    cots = []

    def send_cot(d):
        for cc in range(2):
            cols = slice(768 * cc, 768 * cc + 768)
            cp = rcopy(cotr.at[my_tok, cols], cotr.at[my_tok, cols], ss_c.at[2 * d - 2 + cc], rs_c.at[2 * d - 2 + core],
                       ctx(y, x + d, cc))
            cp.start()
            cots.append(cp)

    send_cot(1)
    send_cot(3)

    sends = []
    osib = []
    ocross = []
    for i, e in enumerate((1, 3)):
        cols = slice(768 * i, 768 * i + 768)
        cp = rcopy(wof.at[wo_rows, cols], wof.at[wo_rows, cols], ss_p.at[i], rs_p.at[i], ring_dev(e))
        cp.start()
        ocross.append(cp)
    wrows = pl.ds(_al(core * 192, 16), 192)
    for j in range(12):
        cols = slice(128 * j, 128 * j + 128)
        wt[wrows, cols] = (qkvt_ref[:, cols].astype(F32) * gain_ref[j : j + 1, :]).astype(BF)
    wcopy = rcopy(wt.at[wrows], wt.at[wrows], ss_w, rs_w, sib)
    wcopy.start()
    cp = rcopy(wof.at[wo_rows], wof.at[wo_rows], ss_q.at[0], rs_q.at[0], sib)
    cp.start()
    osib.append(cp)
    csib = [rcopy(cotr.at[my_tok], cotr.at[my_tok], ss_d.at[0], rs_d.at[0], sib)]
    csib[0].start()

    lax.fori_loop(2, 3, comp, 0)
    for b in range(4):
        for j in range(6):
            wcp[128 * b : 128 * b + 128, 128 * j : 128 * j + 128] = wc[j, pl.ds(b, 128, stride=4), :].astype(BF)
    yb[0:8, :] = jnp.zeros((8, 768), F32)
    yb[1288:1296, :] = jnp.zeros((8, 768), F32)
    bsc[...] = jnp.zeros((8, 128), F32)
    bsc[0:1, 0:96] = convb_ref[...]
    for cp in bsib:
        cp.wait_recv()

    def taps(i, c):
        rows = pl.ds(_al(i * 256, 256), 256)
        bb = ball[rows, :].astype(F32)
        for b in range(4):
            oh[:, 128 * b : 128 * b + 128] = jnp.where(bb == float(b), 1.0, 0.0).astype(BF)
        yb[pl.ds(_al(i * 256 + 8, 8), 256), :] = _dot(oh[...], wcp[...])
        return c


    bias = jnp.broadcast_to(bsc[0:1, :], (128, 128)).T[0:96]

    def act(q, c):
        win = pl.ds(_al(q * 128, 8), 144)
        pre = jnp.zeros((128, 128), F32)
        for j in range(5):
            pre = pre + yb[win, 128 * j : 128 * j + 128][6 + j : 134 + j]
        own = yb[pl.ds(_al(q * 128 + 8, 8), 128), 640:768]
        val = own.T[0:96] + _gelu(pre.T[0:96] + bias)
        st[q // 5, :, pl.ds(_al(lax.rem(q, 5) * 128, 128), 128)] = val.astype(BF)
        return c

    own_rows = pl.ds(_al(me * 96, 16), 96)

    def s1(rel, ct):
        to = ctx(y, x + rel + 1, ct) if rel < 3 else ctx(1 - y, x, ct)
        return rcopy(st.at[ct], xt.at[own_rows], ss1.at[rel * 2 + ct], rs1.at[rel * 2 + core], to)

    for half in range(2):
        lax.fori_loop(3 * half, 3 + 2 * half, taps, 0)
        lax.fori_loop(5 * half, 5 * half + 5, act, 0)
        for rel in (3, 0, 2, 1):
            cp = s1(rel, half)
            cp.start()
            sends.append(cp)

        @pl.when(core == half)
        def _():
            xt[own_rows, :] = st[half]

        @pl.when(core != half)
        def _():
            rcopy(st.at[half], xt.at[own_rows], ss1.at[8], rs1.at[8], sib).start()

    def chip_rows(kk):
        return pl.ds(_al(kk * 192, 16), 192)

    def s1_wait(rel):
        for cs in range(2):
            rcopy(st.at[0], xt.at[own_rows], ss1.at[rel * 2 + cs], rs1.at[rel * 2 + cs], sib).wait_recv()

    s1_wait(3)
    ky = (1 - y) * 4 + x
    for d in (1, 3, 2):
        src = xt.at[chip_rows(ky), LA:640]
        cp = rcopy(src, src, ss2.at[2 + d], rs2.at[2 + d], ctx(y, x + d, core))
        cp.start()
        sends.append(cp)
    for d in (1, 3, 2):
        s1_wait(d - 1)
        src = xt.at[chip_rows(y * 4 + lax.rem(x + 4 - d, 4)), 0:LA]
        cp = rcopy(src, src, ss2.at[d - 1], rs2.at[d - 1], ctx(1 - y, x, core))
        cp.start()
        sends.append(cp)

    send_cot(2)

    def cot_to_sib(d):
        for cs in range(2):
            rcopy(cotr.at[my_tok, 0:768], cotr.at[my_tok, 0:768], ss_c.at[0], rs_c.at[2 * d - 2 + cs], sib).wait_recv()
        part = cotr.at[pl.ds(_al(lax.rem(x + 4 - d, 4) * 160, 16), 160), pl.ds(_al(core * 768, 128), 768)]
        cp = rcopy(part, part, ss_d.at[d], rs_d.at[d], sib)
        cp.start()
        csib.append(cp)

    cot_to_sib(1)
    cot_to_sib(3)
    for cp in ocross:
        cp.wait_recv()
    cp = rcopy(wof.at[wo_other], wof.at[wo_other], ss_q.at[1], rs_q.at[1], sib)
    cp.start()
    osib.append(cp)
    ox = []
    for d in (1, 3, 2):
        for cc in range(2):
            for w, orows in enumerate((wo_rows, wo_other)):
                part = wof.at[orows, 768 * cc : 768 * cc + 768]
                i = (2 * d - 2) * 2 + w
                cp = rcopy(part, part, ss_o.at[i + 2 * cc], rs_o.at[i + 2 * core], ctx(y, x + d, cc))
                cp.start()
                ox.append(cp)

    wcopy.wait()
    rcopy(st.at[0], xt.at[own_rows], ss1.at[8], rs1.at[8], sib).wait_recv()

    def sq(i, tot):
        v = xt[pl.ds(_al(i * 128, 128), 128), :].astype(F32)
        return tot + jnp.sum((v * v).reshape(16, 8, 640), axis=0)

    def part(h, lo, hi, row):
        return _dot(wt[192 * h + lo : 192 * h + hi, pl.ds(_al(row * 768, 128), 768)], xt[pl.ds(_al(row * 768, 16), 768), :])

    total = lax.fori_loop(y * 6, y * 6 + 6, sq, jnp.zeros((8, 640), F32))
    for h in range(2):
        acc[h] = part(h, 0, 192, y)
    for d in (1, 3, 2):
        src = xt.at[chip_rows(0), LA:640]
        rcopy(src, src, ss2.at[2 + d], rs2.at[2 + d], sib).wait_recv()
        src = xt.at[chip_rows(0), 0:LA]
        rcopy(src, src, ss2.at[d - 1], rs2.at[d - 1], sib).wait_recv()
    total = lax.fori_loop(6 - y * 6, 12 - y * 6, sq, total)
    scale = lax.rsqrt(jnp.sum(total, axis=0, keepdims=True) * (1.0 / 1536.0) + 1e-06)
    kcopy = []
    for h in range(2):
        kv[core, h] = ((acc[h, 64:192] + part(h, 64, 192, 1 - y)) * scale).astype(BF)
        cp = rcopy(kv.at[core, h], kv.at[core, h], ss_k.at[h], rs_k.at[h], sib)
        cp.start()
        kcopy.append(cp)
    for h in range(2):
        qt[h] = ((acc[h, 0:64] + part(h, 0, 64, 1 - y)) * scale * 0.125).astype(BF)

    scopy = rcopy(sbuf.at[1 - core], sown, ss_s, rs_s, sib)

    @pl.when(core == y)
    def _():
        r = lax.broadcasted_iota(jnp.int32, (160, 640), 0) + 160 * x
        cidx = lax.broadcasted_iota(jnp.int32, (160, 640), 1)
        pick = jnp.where(r == cidx, 1.0, 0.0).astype(BF)
        for n in range(6):
            part = lax.dot_general(pick, xt[256 * n : 256 * n + 256, :], (((1,), (1,)), ((), ())),
                                   preferred_element_type=F32).astype(BF)
            sbuf[0, :, 256 * n : 256 * n + 256] = part[0:80]
            sbuf[1, :, 256 * n : 256 * n + 256] = part[80:160]
        sown[...] = sbuf[core]
        scopy.start()

    for cp in kcopy:
        cp.wait()
    for h in range(2):
        for half in range(2):
            ks[h, 640 * half : 640 * half + 640, :] = kv[half, h, 0:64, :].astype(F32).T.astype(BF)

    steps = [(h, a, w) for a, w in ((0, 256), (256, 256), (512, 128)) for h in range(2)]

    def score(n):
        h, a, w = steps[n]
        sc[n % 2, :, 0:w] = _dot(ks[h], qt[h, :, a : a + w])

    kx = core * 4 + x
    trows = pl.ds(_al(y * 64, 16), 64)
    tiles = ((0, 256), (256, 256), (512, 128))

    def tcopy(t, cc):
        a, w = tiles[t]
        return rcopy(at.at[64 * cc : 64 * cc + 64, a : a + w], ath.at[trows, a : a + w], ss_t.at[2 * t + cc],
                     rs_t.at[2 * t + y], kx * 2 + cc)

    def acopy(j):
        return rcopy(an.at[80 * j : 80 * j + 80], aown.at[:, pl.ds(_al(chip * 128, 128), 128)], ss_a.at[j], rs_a.at[chip],
                     8 * core + j)

    score(0)
    outs = [None, None]
    for n, (h, a, w) in enumerate(steps):
        if n + 1 < len(steps):
            score(n + 1)
        s = sc[n % 2, :, 0:w]
        p = jnp.exp(s - jnp.max(s, axis=0, keepdims=True))
        den = jnp.sum(p, axis=0, keepdims=True)
        pb = p.astype(BF)
        o = (_dot(kv[0, h, 64:128, :], pb[0:640]) + _dot(kv[1, h, 64:128, :], pb[640:1280])) / den
        at[64 * h : 64 * h + 64, a : a + w] = o.astype(BF)
        outs[h] = o
        if h == 1:
            t = n // 2
            for cc in range(2):
                @pl.when(kx * 2 + cc == me)
                def _():
                    ath[trows, a : a + w] = at[64 * cc : 64 * cc + 64, a : a + w]

                @pl.when(kx * 2 + cc != me)
                def _():
                    tcopy(t, cc).start()
            an[a : a + w, :] = jnp.concatenate(outs, axis=0).T.astype(BF)
            for j in ((0, 1, 2), (3, 4, 5), (6, 7))[t]:
                @pl.when(8 * core + j == me)
                def _():
                    aown[:, pl.ds(_al(chip * 128, 128), 128)] = an[80 * j : 80 * j + 80, :]

                @pl.when(8 * core + j != me)
                def _():
                    acopy(j).start()

    cot_to_sib(2)

    def t_wait(yy):
        for t in range(3):
            a, w = tiles[t]
            rcopy(at.at[0:64, a : a + w], ath.at[0:64, a : a + w], ss_t.at[0], rs_t.at[2 * t + yy], sib).wait_recv()

    t_wait(1 - y)

    @pl.when(core != y)
    def _():
        t_wait(y)

    for cp in csib:
        cp.wait_recv()

    def block(r, i):
        return pl.ds(_al(lax.rem(r, 2) * 64, 16), 64), pl.ds(_al((r // 2) * 768 + 384 * i, 128), 384)

    ysend, nsend, fsend, gsend = [[], []], [[], []], [[], []], [[], []]
    for i in range(2):
        for hh in range(2):
            cols = slice(768 * hh + 384 * i, 768 * hh + 384 * i + 384)
            gl[:, cols] = _dot(ath[...], cotr[:, cols]).astype(BF)
        for e in (1, 3, 2):
            rows, cols = block(lax.rem(ring + e, 4), i)
            k = 3 * i + e - 1
            cp = rcopy(gl.at[rows, cols], yr.at[k], ss_y.at[k], rs_y.at[k], ring_dev(e))
            cp.start()
            ysend[i].append(cp)

    for i in range(2):
        rows, cols = block(ring, i)
        acc = gl[rows, cols].astype(F32)
        for e, cp in zip((1, 3, 2), ysend[i]):
            cp.wait_recv()
            acc = acc + yr[3 * i + e - 1].astype(F32)
        zs[i] = acc.astype(BF)
        for e in (1, 3, 2):
            k = 3 * i + e - 1
            cp = rcopy(zs.at[i, pl.ds(_al(lax.rem(zb + e, 4) * 16, 16), 16)], nr.at[k], ss_n.at[k], rs_n.at[k], near(e))
            cp.start()
            nsend[i].append(cp)
    zrows = pl.ds(_al(zb * 16, 16), 16)
    for i in range(2):
        acc = zs[i, zrows, :].astype(F32)
        for e, cp in zip((1, 3, 2), nsend[i]):
            cp.wait_recv()
            acc = acc + nr[3 * i + e - 1].astype(F32)
        fr[i, za] = acc.astype(BF)
        for e in (2, 1, 3):
            k = 3 * i + e - 1
            cp = rcopy(fr.at[i, za], fr.at[i, za], ss_f.at[k], rs_f.at[k], far(e))
            cp.start()
            fsend[i].append(cp)
    for i in range(2):
        for cp in fsend[i]:
            cp.wait_recv()
        acc = fr[i, 0].astype(F32)
        for q in range(1, 4):
            acc = acc + fr[i, q].astype(F32)
        rc[i] = acc.astype(BF)
        fcols = pl.ds(_al(yh * 768 + 384 * i, 128), 384)
        fb[zrows, fcols] = rc[i]
        for k, to in enumerate([across(e) for e in range(4)] + [near(e) for e in (1, 2, 3)]):
            cp = rcopy(rc.at[i], fb.at[zrows, fcols], ss_g.at[7 * i + k], rs_g.at[7 * i + k], to)
            cp.start()
            gsend[i].append(cp)

    wo_cols = pl.ds(_al(core * 768, 128), 768)
    for d in (1, 3, 2):
        for i in range(4):
            rcopy(wof.at[0:64, 0:768], wof.at[0:64, 0:768], ss_o.at[0], rs_o.at[(2 * d - 2) * 2 + i], sib).wait_recv()
        for yy in range(2):
            part = wof.at[pl.ds(_al((yy * 4 + lax.rem(x + 4 - d, 4)) * 128, 16), 128), wo_cols]
            k = 2 + (d - 1) * 2 + yy
            cp = rcopy(part, part, ss_q.at[k], rs_q.at[k], sib)
            cp.start()
            osib.append(cp)
    for k in range(8):
        @pl.when(2 * k + y != me)
        def _():
            rcopy(an.at[0:80], aown.at[:, 0:128], ss_a.at[0], rs_a.at[k], sib).wait_recv()

    @pl.when(core != y)
    def _():
        scopy.wait_recv()

    for cp in osib:
        cp.wait_recv()
    for n in range(6):
        cols = slice(256 * n, 256 * n + 256)
        out_ref[:, cols] = (sown[:, cols].astype(F32) + _dot(aown[...], wof[:, cols])).astype(BF)

    for i in range(2):
        for cp in gsend[i]:
            cp.wait_recv()
    grad_ref[...] = fb[...]

    @pl.when(core == y)
    def _():
        scopy.wait_send()

    for cp in sends + bplane + bsib + ocross + osib + ox + cots + csib:
        cp.wait_send()
    for i in range(2):
        for cp in ysend[i] + nsend[i] + fsend[i] + gsend[i]:
            cp.wait_send()
    rcopy(st.at[0], xt.at[own_rows], ss1.at[8], rs1.at[8], sib).wait_send()
    for cc in range(2):
        @pl.when(kx * 2 + cc != me)
        def _():
            for t in range(3):
                tcopy(t, cc).wait_send()
    for j in range(8):
        @pl.when(8 * core + j != me)
        def _():
            acopy(j).wait_send()


def place_kernel(a_ref, b_ref, oa_ref, ob_ref):
    oa_ref[...] = a_ref[...]
    ob_ref[...] = b_ref[...]


def per_device(bases, embed_w, conv_w, conv_b, norm_g, qkv_w, wo, cotangent):
    vm = pl.BlockSpec(memory_space=pltpu.VMEM)
    V = pltpu.VMEM

    def sems(n):
        return [pltpu.SemaphoreType.DMA((n,)), pltpu.SemaphoreType.DMA((n,))]

    one = [pltpu.SemaphoreType.DMA, pltpu.SemaphoreType.DMA]
    out, wo_grad = pl.pallas_call(
        layer_kernel,
        out_shape=(jax.ShapeDtypeStruct((80, 1536), BF), jax.ShapeDtypeStruct((64, 1536), BF)),
        in_specs=[pl.BlockSpec(memory_space=pltpu.HBM)] * 8,
        out_specs=(vm,) * 2,
        scratch_shapes=[
            V((1280, 128), BF), V((8, 128), F32), V((768, 1536), BF), V((6, 512, 128), F32), V((512, 768), BF),
            V((256, 512), BF), V((1296, 768), F32), V((2, 96, 640), BF), V((1536, 640), BF), V((384, 1536), BF),
            V((2, 64, 640), BF), V((2, 2, 128, 640), BF), V((2, 1280, 64), BF), V((2, 1280, 256), F32),
            V((128, 640), BF), V((640, 128), BF), V((128, 640), BF), V((80, 1024), BF), V((2, 80, 1536), BF),
            V((80, 1536), BF), V((640, 1536), BF), V((1024, 1536), BF),
            V((128, 1536), BF), V((6, 64, 384), BF), V((2, 64, 384), BF), V((6, 16, 384), BF), V((2, 4, 16, 384), BF),
            V((2, 16, 384), BF), V((64, 1536), BF), V((2, 192, 640), F32),
            V((80, 128), jnp.int32), V((512, 1536), BF), V((1, 96), F32), V((192, 1536), BF), V((12, 128), F32),
            pltpu.SemaphoreType.DMA((12,)),
        ] + sems(15) + one + sems(9) + sems(6) + sems(6) + sems(2) + one + sems(6) + sems(8) + sems(4) + sems(12) + sems(2)
        + sems(8) + sems(6) + sems(6) + sems(6) + sems(14),
        compiler_params=pltpu.CompilerParams(collective_id=0, has_side_effects=True, vmem_limit_bytes=56 << 20),
        name="layer",
    )(bases.reshape(80, 128), embed_w, conv_w.transpose(0, 2, 1).reshape(480, 1536), conv_b[None], qkv_w.T,
      norm_g.reshape(12, 128), wo, cotangent[0])
    out, wo_grad = pl.pallas_call(
        place_kernel,
        out_shape=(jax.ShapeDtypeStruct((80, 1536), BF), jax.ShapeDtypeStruct((64, 1536), BF)),
        in_specs=[vm] * 2,
        out_specs=(vm,) * 2,
        name="place",
    )(out, wo_grad)
    return out[None], wo_grad


def solution(mesh):
    return jax.shard_map(
        per_device,
        mesh=mesh,
        in_specs=(
            P("dp", "ctx"), P(), P(None, None, "ctx"), P("ctx"), P(), P(None, "ctx"), P("ctx", None),
            P("dp", "ctx", None),
        ),
        out_specs=(P("dp", "ctx", None), P("ctx", None)),
        check_vma=False,
    )
```

```python
import functools

import jax
import jax.numpy as jnp
from jax import lax
from jax.experimental import pallas as pl
from jax.experimental.pallas import tpu as pltpu
from jax.sharding import PartitionSpec as P

MESH = pl.DeviceIdType.MESH
BF = jnp.bfloat16
F32 = jnp.float32
LA = 256


def _al(v, m):
    return pl.multiple_of(v, m)


def _dot(a, b):
    return jnp.dot(a, b, preferred_element_type=F32)


def _gelu(v):
    return 0.5 * v * (1.0 + jnp.tanh(0.7978845608028654 * (v + 0.044715 * (v * v * v))))


def layer_kernel(
    bases_hbm, embed_hbm, convt_hbm, convb_hbm, qkvt_hbm, gain_hbm, wo_hbm, cot_hbm,
    out_ref, grad_ref,
    ball, bsc, wcat, wc, wcp, oh, yb, st, xt, wt, qt, kv, ks, sc, at, an, ath, aown, sbuf, sown, cotr, wof,
    pbuf, prx, pown, obuf, orx,
    gl, yr, zs, nr, fr, rc, fb, acc, bases_ref, embed_ref, convb_ref, qkvt_ref, gain_ref, ld,
    ss_b, rs_b, ss_w, rs_w, ss1, rs1, ss2, rs2, ss_c, rs_c, ss_k, rs_k, ss_s, rs_s, ss_t, rs_t, ss_a, rs_a,
    ss_d, rs_d, ss_o, rs_o, ss_p, rs_p, ss_q, rs_q, ss3, rs3, ss4, rs4, ss_y, rs_y, ss_n, rs_n, ss_f, rs_f, ss_g, rs_g,
):
    dp = lax.axis_index("dp")
    me = lax.axis_index("ctx")
    yh, z = dp // 16, lax.rem(dp, 16)
    za, zb = z // 4, lax.rem(z, 4)
    core = lax.rem(me, 2)
    chip = me // 2
    x = lax.rem(chip, 4)
    y = me // 8
    sib = me + 1 - 2 * core
    ring = 2 * yh + y

    def ctx(yy, xx, cc):
        return (yy * 4 + lax.rem(xx, 4)) * 2 + cc

    def rcopy(src, dst, ssem, rsem, to):
        return pltpu.make_async_remote_copy(
            src_ref=src, dst_ref=dst, send_sem=ssem, recv_sem=rsem,
            device_id=to if isinstance(to, tuple) else (dp, to), device_id_type=MESH,
        )

    def ring_dev(e):
        r = lax.rem(ring + e, 4)
        return (r // 2) * 16 + z, lax.rem(r, 2) * 8 + lax.rem(me, 8)

    def near(e):
        return yh * 16 + za * 4 + lax.rem(zb + e, 4), me

    def across(e):
        return (1 - yh) * 16 + za * 4 + lax.rem(zb + e, 4), me

    def far(e):
        return yh * 16 + lax.rem(za + e, 4) * 4 + zb, me

    wo_rows = pl.ds(_al(lax.rem(me, 8) * 64, 16), 64)
    my_tok = pl.ds(_al(lax.rem(me, 8) * 80, 16), 80)
    barrier = pltpu.get_barrier_semaphore()
    greet = [(dp, lax.rem(me + d, 16)) for d in range(1, 16)]
    greet += [near(e) for e in (1, 2, 3)] + [far(e) for e in (1, 2, 3)] + [across(e) for e in range(4)]
    greet += [((1 - yh) * 16 + z, (1 - y) * 8 + lax.rem(me, 8))]
    for to in greet:
        pl.semaphore_signal(barrier, inc=1, device_id=to, device_id_type=MESH)
    loads = [
        pltpu.make_async_copy(src, dst, ld.at[i])
        for i, (src, dst) in enumerate(
            [(bases_hbm, bases_ref), (embed_hbm, embed_ref)]
            + [(convt_hbm.at[96 * j : 96 * j + 96], wcat.at[128 * j : 128 * j + 96]) for j in range(5)]
            + [(qkvt_hbm, qkvt_ref), (gain_hbm, gain_ref), (convb_hbm, convb_ref)]
            + [(wo_hbm, wof.at[wo_rows]), (cot_hbm, cotr.at[my_tok])]
        )
    ]
    for cp in loads:
        cp.start()
    loads[0].wait()
    ball[pl.ds(_al(me * 80, 16), 80), :] = bases_ref[...].astype(F32).astype(BF)
    pl.semaphore_wait(barrier, len(greet))

    plane = [(0, 1), (0, 3), (1, 0), (1, 1), (1, 3), (0, 2), (1, 2)]

    def ball_of(dev):
        return ball.at[pl.ds(_al(dev * 80, 16), 80)]

    def ysel(dy):
        return y + dy - 2 * dy * y

    bplane = []
    for i, (dy, dx) in enumerate(plane):
        cp = rcopy(ball_of(me), ball_of(me), ss_b.at[i], rs_b.at[i], ctx(ysel(dy), x + dx, core))
        cp.start()
        bplane.append(cp)
    bsib = [rcopy(ball_of(me), ball_of(me), ss_b.at[7], rs_b.at[7], sib)]
    bsib[0].start()

    for j in range(6):
        wcat[128 * j + 96 : 128 * j + 128, :] = jnp.zeros((32, 1536), BF)
    r = lax.broadcasted_iota(jnp.int32, (96, 1536), 0) + 96 * me
    cc = lax.broadcasted_iota(jnp.int32, (96, 1536), 1)
    wcat[640:736, :] = jnp.where(r == cc, 1.0, 0.0).astype(BF)
    for cp in loads[1:7]:
        cp.wait()

    def comp(i, c):
        prod = lax.dot_general(embed_ref[...], wcat[pl.ds(_al(i * 256, 256), 256), :], (((1,), (1,)), ((), ())),
                               preferred_element_type=F32)
        wc[2 * i] = prod[:, 0:128]
        wc[2 * i + 1] = prod[:, 128:256]
        return c

    lax.fori_loop(0, 2, comp, 0)
    for i, (dy, dx) in enumerate(plane):
        bplane[i].wait_recv()
        src = ball_of(ctx(ysel(dy), x + 4 - dx, core))
        cp = rcopy(src, src, ss_b.at[8 + i], rs_b.at[8 + i], sib)
        cp.start()
        bsib.append(cp)

    for cp in loads[7:12]:
        cp.wait()

    cots = []

    def send_cot(d):
        for cc in range(2):
            cols = slice(768 * cc, 768 * cc + 768)
            cp = rcopy(cotr.at[my_tok, cols], cotr.at[my_tok, cols], ss_c.at[2 * d - 2 + cc], rs_c.at[2 * d - 2 + core],
                       ctx(y, x + d, cc))
            cp.start()
            cots.append(cp)

    send_cot(1)
    send_cot(3)

    sends = []
    wrows = pl.ds(_al(core * 192, 16), 192)
    for j in range(12):
        cols = slice(128 * j, 128 * j + 128)
        wt[wrows, cols] = (qkvt_ref[:, cols].astype(F32) * gain_ref[j : j + 1, :]).astype(BF)
    wcopy = rcopy(wt.at[wrows], wt.at[wrows], ss_w, rs_w, sib)
    wcopy.start()
    for cc in range(2):
        cols = slice(768 * cc, 768 * cc + 768)

        @pl.when(core != cc)
        def _():
            rcopy(wof.at[wo_rows, cols], wof.at[wo_rows, cols], ss_o.at[6], rs_o.at[6], sib).start()

    csib = [rcopy(cotr.at[my_tok], cotr.at[my_tok], ss_d.at[0], rs_d.at[0], sib)]
    csib[0].start()

    lax.fori_loop(2, 3, comp, 0)
    for b in range(4):
        for j in range(6):
            wcp[128 * b : 128 * b + 128, 128 * j : 128 * j + 128] = wc[j, pl.ds(b, 128, stride=4), :].astype(BF)
    yb[0:8, :] = jnp.zeros((8, 768), F32)
    yb[1288:1296, :] = jnp.zeros((8, 768), F32)
    bsc[...] = jnp.zeros((8, 128), F32)
    bsc[0:1, 0:96] = convb_ref[...]
    for cp in bsib:
        cp.wait_recv()

    def taps(i, c):
        rows = pl.ds(_al(i * 256, 256), 256)
        bb = ball[rows, :].astype(F32)
        for b in range(4):
            oh[:, 128 * b : 128 * b + 128] = jnp.where(bb == float(b), 1.0, 0.0).astype(BF)
        yb[pl.ds(_al(i * 256 + 8, 8), 256), :] = _dot(oh[...], wcp[...])
        return c


    bias = jnp.broadcast_to(bsc[0:1, :], (128, 128)).T[0:96]

    def act(q, c):
        win = pl.ds(_al(q * 128, 8), 144)
        pre = jnp.zeros((128, 128), F32)
        for j in range(5):
            pre = pre + yb[win, 128 * j : 128 * j + 128][6 + j : 134 + j]
        own = yb[pl.ds(_al(q * 128 + 8, 8), 128), 640:768]
        val = own.T[0:96] + _gelu(pre.T[0:96] + bias)
        st[q // 5, :, pl.ds(_al(lax.rem(q, 5) * 128, 128), 128)] = val.astype(BF)
        return c

    own_rows = pl.ds(_al(me * 96, 16), 96)

    def s1(rel, ct):
        to = ctx(y, x + rel + 1, ct) if rel < 3 else ctx(1 - y, x, ct)
        return rcopy(st.at[ct], xt.at[own_rows], ss1.at[rel * 2 + ct], rs1.at[rel * 2 + core], to)

    for half in range(2):
        lax.fori_loop(3 * half, 3 + 2 * half, taps, 0)
        lax.fori_loop(5 * half, 5 * half + 5, act, 0)
        for rel in (3, 0, 2):
            cp = s1(rel, half)
            cp.start()
            sends.append(cp)

        @pl.when(core == half)
        def _():
            xt[own_rows, :] = st[half]

        @pl.when(core != half)
        def _():
            rcopy(st.at[half], xt.at[own_rows], ss1.at[8], rs1.at[8], sib).start()

    def chip_rows(kk):
        return pl.ds(_al(kk * 192, 16), 192)

    def s1_wait(rel):
        for cs in range(2):
            rcopy(st.at[0], xt.at[own_rows], ss1.at[rel * 2 + cs], rs1.at[rel * 2 + cs], sib).wait_recv()

    def chip_at(yy, d):
        return yy * 4 + lax.rem(x + d, 4)

    def push(ref, ssem, rsem, to):
        cp = rcopy(ref, ref, ssem, rsem, to)
        cp.start()
        sends.append(cp)

    def to_y(d):
        push(xt.at[chip_rows(chip_at(y, 4 - d)), 0:LA], ss2.at[d - 1], rs2.at[d - 1], ctx(1 - y, x, core))

    def half_rows(kk, i):
        return pl.ds(_al(kk * 192 + 96 * i, 16), 96)

    s1_wait(3)
    for d in (1, 3):
        push(xt.at[chip_rows(chip_at(1 - y, 0)), LA:640], ss2.at[2 + d], rs2.at[2 + d], ctx(y, x + d, core))
    for i, d in ((0, 1), (1, 3)):
        s1_wait(d - 1)
        to_y(d)
        push(xt.at[half_rows(chip_at(y, 4 - d), i)], ss3.at[i], rs3.at[i], ctx(y, x + d, core))
    for i in range(2):
        rcopy(st.at[0], xt.at[own_rows], ss3.at[i], rs3.at[i], sib).wait_recv()
    to_y(2)
    for i, d in ((0, 1), (1, 3)):
        src = xt.at[chip_rows(0), LA:640]
        rcopy(src, src, ss2.at[2 + d], rs2.at[2 + d], sib).wait_recv()
        push(xt.at[half_rows(chip_at(1 - y, 4 - d), i), LA:640], ss4.at[i], rs4.at[i], ctx(y, x + d, core))

    core_cols = pl.ds(_al(core * 768, 128), 768)

    def cot_rows(d, i, n):
        return pl.ds(_al(lax.rem(x + 4 - d, 4) * 160 + 80 * i, 16), n)

    def cot_to_sib(d):
        part = cotr.at[cot_rows(d, 0, 160), core_cols]
        cp = rcopy(part, part, ss_d.at[d], rs_d.at[d], sib)
        cp.start()
        csib.append(cp)

    for i, d in ((0, 1), (1, 3)):
        for cs in range(2):
            rcopy(cotr.at[my_tok, 0:768], cotr.at[my_tok, 0:768], ss_c.at[0], rs_c.at[2 * d - 2 + cs], sib).wait_recv()
        part = cotr.at[cot_rows(d, i, 80), core_cols]
        cp = rcopy(part, part, ss_c.at[2 + i], rs_c.at[2 + i], ctx(y, x + d, core))
        cp.start()
        cots.append(cp)
        cot_to_sib(d)
    for d in (1, 3, 2):
        for cc in range(2):
            part = wof.at[wo_rows, 768 * cc : 768 * cc + 768]
            cp = rcopy(part, part, ss_o.at[2 * d - 2 + cc], rs_o.at[2 * d - 2 + core], ctx(y, x + d, cc))
            cp.start()
            sends.append(cp)

    wcopy.wait()
    rcopy(st.at[0], xt.at[own_rows], ss1.at[8], rs1.at[8], sib).wait_recv()

    def sq(i, tot):
        v = xt[pl.ds(_al(i * 128, 128), 128), :].astype(F32)
        return tot + jnp.sum((v * v).reshape(16, 8, 640), axis=0)

    def part(h, lo, hi, row):
        return _dot(wt[192 * h + lo : 192 * h + hi, pl.ds(_al(row * 768, 128), 768)], xt[pl.ds(_al(row * 768, 16), 768), :])

    total = lax.fori_loop(y * 6, y * 6 + 6, sq, jnp.zeros((8, 640), F32))
    for h in range(2):
        acc[h] = part(h, 0, 192, y)
    for d in (1, 3, 2):
        src = xt.at[chip_rows(0), 0:LA]
        rcopy(src, src, ss2.at[d - 1], rs2.at[d - 1], sib).wait_recv()
    for i in range(2):
        src = xt.at[own_rows, LA:640]
        rcopy(src, src, ss4.at[i], rs4.at[i], sib).wait_recv()
    total = lax.fori_loop(6 - y * 6, 12 - y * 6, sq, total)
    scale = lax.rsqrt(jnp.sum(total, axis=0, keepdims=True) * (1.0 / 1536.0) + 1e-06)
    kcopy = []
    for h in range(2):
        kv[core, h] = ((acc[h, 64:192] + part(h, 64, 192, 1 - y)) * scale).astype(BF)
        cp = rcopy(kv.at[core, h], kv.at[core, h], ss_k.at[h], rs_k.at[h], sib)
        cp.start()
        kcopy.append(cp)
    for h in range(2):
        qt[h] = ((acc[h, 0:64] + part(h, 0, 64, 1 - y)) * scale * 0.125).astype(BF)

    scopy = rcopy(sbuf.at[1 - core], sown, ss_s, rs_s, sib)

    @pl.when(core == y)
    def _():
        r = lax.broadcasted_iota(jnp.int32, (160, 640), 0) + 160 * x
        cidx = lax.broadcasted_iota(jnp.int32, (160, 640), 1)
        pick = jnp.where(r == cidx, 1.0, 0.0).astype(BF)
        for n in range(6):
            sbuf[n // 3, :, 256 * (n % 3) : 256 * (n % 3) + 256] = lax.dot_general(
                pick, xt[256 * n : 256 * n + 256, :], (((1,), (1,)), ((), ())), preferred_element_type=F32).astype(BF)
        sown[...] = sbuf[core]
        scopy.start()

    for cp in kcopy:
        cp.wait()
    for h in range(2):
        for half in range(2):
            ks[h, 640 * half : 640 * half + 640, :] = kv[half, h, 0:64, :].astype(F32).T.astype(BF)

    steps = [(h, a, w) for a, w in ((0, 256), (256, 256), (512, 128)) for h in range(2)]

    def score(n):
        h, a, w = steps[n]
        sc[n % 2, :, 0:w] = _dot(ks[h], qt[h, :, a : a + w])

    kx = core * 4 + x
    trows = pl.ds(_al(y * 64, 16), 64)
    tiles = ((0, 256), (256, 256), (512, 128))

    def tcopy(t, cc):
        a, w = tiles[t]
        return rcopy(at.at[64 * cc : 64 * cc + 64, a : a + w], ath.at[trows, a : a + w], ss_t.at[2 * t + cc],
                     rs_t.at[2 * t + y], kx * 2 + cc)

    def acopy(d, cc):
        return rcopy(an.at[pl.ds(_al(lax.rem(x + d, 4) * 160, 16), 160)], aown.at[a_rows, a_cols], ss_a.at[2 * d + cc],
                     rs_a.at[2 * d + core], ctx(y, x + d, cc))

    a_rows = pl.ds(_al(core * 160, 16), 160)
    a_cols = pl.ds(_al(x * 128, 128), 128)

    score(0)
    outs = [None, None]
    for n, (h, a, w) in enumerate(steps):
        if n + 1 < len(steps):
            score(n + 1)
        s = sc[n % 2, :, 0:w]
        p = jnp.exp(s - jnp.max(s, axis=0, keepdims=True))
        den = jnp.sum(p, axis=0, keepdims=True)
        pb = p.astype(BF)
        o = (_dot(kv[0, h, 64:128, :], pb[0:640]) + _dot(kv[1, h, 64:128, :], pb[640:1280])) / den
        at[64 * h : 64 * h + 64, a : a + w] = o.astype(BF)
        outs[h] = o
        if h == 1:
            t = n // 2
            for cc in range(2):
                @pl.when(kx * 2 + cc == me)
                def _():
                    ath[trows, a : a + w] = at[64 * cc : 64 * cc + 64, a : a + w]

                @pl.when(kx * 2 + cc != me)
                def _():
                    tcopy(t, cc).start()
            an[a : a + w, :] = jnp.concatenate(outs, axis=0).T.astype(BF)

    aown[a_rows, a_cols] = an[pl.ds(_al(x * 160, 16), 160), :]
    for d in (1, 3, 2):
        for cc in range(2):
            acopy(d, cc).start()
    for cc in range(2):
        @pl.when(core != cc)
        def _():
            acopy(0, cc).start()

    for i in range(2):
        rcopy(cotr.at[my_tok, 0:768], cotr.at[my_tok, 0:768], ss_c.at[0], rs_c.at[2 + i], sib).wait_recv()
    cot_to_sib(2)

    def t_wait(yy):
        for t in range(3):
            a, w = tiles[t]
            rcopy(at.at[0:64, a : a + w], ath.at[0:64, a : a + w], ss_t.at[0], rs_t.at[2 * t + yy], sib).wait_recv()

    t_wait(1 - y)

    @pl.when(core != y)
    def _():
        t_wait(y)

    for cp in csib:
        cp.wait_recv()

    def block(r, i):
        return pl.ds(_al(lax.rem(r, 2) * 64, 16), 64), pl.ds(_al((r // 2) * 768 + 384 * i, 128), 384)

    ysend, nsend, fsend, gsend = [[], []], [[], []], [[], []], [[], []]
    for i in range(2):
        for hh in range(2):
            cols = slice(768 * hh + 384 * i, 768 * hh + 384 * i + 384)
            gl[:, cols] = _dot(ath[...], cotr[:, cols]).astype(BF)
        for e in (1, 3, 2):
            rows, cols = block(lax.rem(ring + e, 4), i)
            k = 3 * i + e - 1
            cp = rcopy(gl.at[rows, cols], yr.at[k], ss_y.at[k], rs_y.at[k], ring_dev(e))
            cp.start()
            ysend[i].append(cp)

    for i in range(2):
        rows, cols = block(ring, i)
        acc = gl[rows, cols].astype(F32)
        for e, cp in zip((1, 3, 2), ysend[i]):
            cp.wait_recv()
            acc = acc + yr[3 * i + e - 1].astype(F32)
        zs[i] = acc.astype(BF)
        for e in (1, 3, 2):
            k = 3 * i + e - 1
            cp = rcopy(zs.at[i, pl.ds(_al(lax.rem(zb + e, 4) * 16, 16), 16)], nr.at[k], ss_n.at[k], rs_n.at[k], near(e))
            cp.start()
            nsend[i].append(cp)
    zrows = pl.ds(_al(zb * 16, 16), 16)
    for i in range(2):
        acc = zs[i, zrows, :].astype(F32)
        for e, cp in zip((1, 3, 2), nsend[i]):
            cp.wait_recv()
            acc = acc + nr[3 * i + e - 1].astype(F32)
        fr[i, za] = acc.astype(BF)
        for e in (2, 1, 3):
            k = 3 * i + e - 1
            cp = rcopy(fr.at[i, za], fr.at[i, za], ss_f.at[k], rs_f.at[k], far(e))
            cp.start()
            fsend[i].append(cp)
    for i in range(7):
        rcopy(wof.at[0:64, 0:768], wof.at[0:64, 0:768], ss_o.at[0], rs_o.at[i], sib).wait_recv()
    for i in range(2, 8):
        rcopy(an.at[0:160], aown.at[0:160, 0:128], ss_a.at[0], rs_a.at[i], sib).wait_recv()
    rcopy(an.at[0:160], aown.at[0:160, 0:128], ss_a.at[0], rs_a.at[1 - core], sib).wait_recv()
    pbuf[...] = _dot(aown[pl.ds(_al((1 - y) * 160, 16), 160), :], wof[:, core_cols]).astype(BF)
    pcopy = rcopy(pbuf, prx, ss_p, rs_p, ctx(1 - y, x, core))
    pcopy.start()
    pown[...] = _dot(aown[pl.ds(_al(y * 160, 16), 160), :], wof[:, core_cols])

    for i in range(2):
        for cp in fsend[i]:
            cp.wait_recv()
        acc = fr[i, 0].astype(F32)
        for q in range(1, 4):
            acc = acc + fr[i, q].astype(F32)
        rc[i] = acc.astype(BF)
        fcols = pl.ds(_al(yh * 768 + 384 * i, 128), 384)
        fb[zrows, fcols] = rc[i]
        for k, to in enumerate([across(e) for e in range(4)] + [near(e) for e in (1, 2, 3)]):
            cp = rcopy(rc.at[i], fb.at[zrows, fcols], ss_g.at[7 * i + k], rs_g.at[7 * i + k], to)
            cp.start()
            gsend[i].append(cp)

    @pl.when(core != y)
    def _():
        scopy.wait_recv()

    pcopy.wait_recv()
    whole = (sown[...].astype(F32) + (pown[...] + prx[...].astype(F32))).astype(BF)
    obuf[0] = whole[0:80]
    obuf[1] = whole[80:160]
    ocopy = rcopy(obuf.at[1 - core], orx, ss_q, rs_q, sib)
    ocopy.start()
    out_ref[:, core_cols] = obuf[core]

    for i in range(2):
        for cp in gsend[i]:
            cp.wait_recv()
    grad_ref[...] = fb[...]
    ocopy.wait_recv()
    out_ref[:, pl.ds(_al(768 - core * 768, 128), 768)] = orx[...]

    @pl.when(core == y)
    def _():
        scopy.wait_send()

    for cp in sends + bplane + bsib + cots + csib + [pcopy, ocopy]:
        cp.wait_send()
    for i in range(2):
        for cp in ysend[i] + nsend[i] + fsend[i] + gsend[i]:
            cp.wait_send()
    rcopy(st.at[0], xt.at[own_rows], ss1.at[8], rs1.at[8], sib).wait_send()
    for cc in range(2):
        @pl.when(kx * 2 + cc != me)
        def _():
            for t in range(3):
                tcopy(t, cc).wait_send()
    for d in (1, 3, 2):
        for cc in range(2):
            acopy(d, cc).wait_send()
    for cc in range(2):
        @pl.when(core != cc)
        def _():
            acopy(0, cc).wait_send()
    rcopy(wof.at[wo_rows, 0:768], wof.at[wo_rows, 0:768], ss_o.at[6], rs_o.at[6], sib).wait_send()


def place_kernel(a_ref, b_ref, oa_ref, ob_ref):
    oa_ref[...] = a_ref[...]
    ob_ref[...] = b_ref[...]


def per_device(bases, embed_w, conv_w, conv_b, norm_g, qkv_w, wo, cotangent):
    vm = pl.BlockSpec(memory_space=pltpu.VMEM)
    V = pltpu.VMEM

    def sems(n):
        return [pltpu.SemaphoreType.DMA((n,)), pltpu.SemaphoreType.DMA((n,))]

    one = [pltpu.SemaphoreType.DMA, pltpu.SemaphoreType.DMA]
    out, wo_grad = pl.pallas_call(
        layer_kernel,
        out_shape=(jax.ShapeDtypeStruct((80, 1536), BF), jax.ShapeDtypeStruct((64, 1536), BF)),
        in_specs=[pl.BlockSpec(memory_space=pltpu.HBM)] * 8,
        out_specs=(vm,) * 2,
        scratch_shapes=[
            V((1280, 128), BF), V((8, 128), F32), V((768, 1536), BF), V((6, 512, 128), F32), V((512, 768), BF),
            V((256, 512), BF), V((1296, 768), F32), V((2, 96, 640), BF), V((1536, 640), BF), V((384, 1536), BF),
            V((2, 64, 640), BF), V((2, 2, 128, 640), BF), V((2, 1280, 64), BF), V((2, 1280, 256), F32),
            V((128, 640), BF), V((640, 128), BF), V((128, 640), BF), V((320, 512), BF), V((2, 160, 768), BF),
            V((160, 768), BF), V((640, 1536), BF), V((512, 1536), BF),
            V((160, 768), BF), V((160, 768), BF), V((160, 768), F32), V((2, 80, 768), BF), V((80, 768), BF),
            V((128, 1536), BF), V((6, 64, 384), BF), V((2, 64, 384), BF), V((6, 16, 384), BF), V((2, 4, 16, 384), BF),
            V((2, 16, 384), BF), V((64, 1536), BF), V((2, 192, 640), F32),
            V((80, 128), jnp.int32), V((512, 1536), BF), V((1, 96), F32), V((192, 1536), BF), V((12, 128), F32),
            pltpu.SemaphoreType.DMA((12,)),
        ] + sems(15) + one + sems(9) + sems(6) + sems(6) + sems(2) + one + sems(6) + sems(8) + sems(4) + sems(7) + one + one
        + sems(2) + sems(2) + sems(6) + sems(6) + sems(6) + sems(14),
        compiler_params=pltpu.CompilerParams(collective_id=0, has_side_effects=True, vmem_limit_bytes=56 << 20),
        name="layer",
    )(bases.reshape(80, 128), embed_w, conv_w.transpose(0, 2, 1).reshape(480, 1536), conv_b[None], qkv_w.T,
      norm_g.reshape(12, 128), wo, cotangent[0])
    out, wo_grad = pl.pallas_call(
        place_kernel,
        out_shape=(jax.ShapeDtypeStruct((80, 1536), BF), jax.ShapeDtypeStruct((64, 1536), BF)),
        in_specs=[vm] * 2,
        out_specs=(vm,) * 2,
        name="place",
    )(out, wo_grad)
    return out[None], wo_grad


def solution(mesh):
    return jax.shard_map(
        per_device,
        mesh=mesh,
        in_specs=(
            P("dp", "ctx"), P(), P(None, None, "ctx"), P("ctx"), P(), P(None, "ctx"), P("ctx", None),
            P("dp", "ctx", None),
        ),
        out_specs=(P("dp", "ctx", None), P("ctx", None)),
        check_vma=False,
    )
```

```python
import functools

import jax
import jax.numpy as jnp
from jax import lax
from jax.experimental import pallas as pl
from jax.experimental.pallas import tpu as pltpu
from jax.sharding import PartitionSpec as P

MESH = pl.DeviceIdType.MESH
BF = jnp.bfloat16
F32 = jnp.float32
LA = 256


def _al(v, m):
    return pl.multiple_of(v, m)


def _dot(a, b):
    return jnp.dot(a, b, preferred_element_type=F32)


def _gelu(v):
    return 0.5 * v * (1.0 + jnp.tanh(0.7978845608028654 * (v + 0.044715 * (v * v * v))))


def layer_kernel(
    bases_hbm, embed_hbm, convt_hbm, convb_hbm, qkvt_hbm, gain_hbm, wo_hbm, cot_hbm,
    out_ref, grad_ref,
    ball, bsc, wcat, wc, wcp, oh, yb, st, xt, wt, qt, kv, ks, sc, at, an, ath, aown, sbuf, sown, cotr, wof,
    pbuf, prx, pown, obuf, orx,
    gl, yr, zs, nr, fr, rc, fb, acc, bases_ref, embed_ref, convb_ref, qkvt_ref, gain_ref, ld,
    ss_b, rs_b, ss_w, rs_w, ss1, rs1, ss2, rs2, ss_c, rs_c, ss_k, rs_k, ss_s, rs_s, ss_t, rs_t, ss_a, rs_a,
    ss_d, rs_d, ss_o, rs_o, ss_p, rs_p, ss_q, rs_q, ss3, rs3, ss4, rs4, ss_y, rs_y, ss_n, rs_n, ss_f, rs_f, ss_g, rs_g,
):
    dp = lax.axis_index("dp")
    me = lax.axis_index("ctx")
    yh, z = dp // 16, lax.rem(dp, 16)
    za, zb = z // 4, lax.rem(z, 4)
    core = lax.rem(me, 2)
    chip = me // 2
    x = lax.rem(chip, 4)
    y = me // 8
    sib = me + 1 - 2 * core
    ring = 2 * yh + y

    def ctx(yy, xx, cc):
        return (yy * 4 + lax.rem(xx, 4)) * 2 + cc

    def rcopy(src, dst, ssem, rsem, to):
        return pltpu.make_async_remote_copy(
            src_ref=src, dst_ref=dst, send_sem=ssem, recv_sem=rsem,
            device_id=to if isinstance(to, tuple) else (dp, to), device_id_type=MESH,
        )

    def ring_dev(e):
        r = lax.rem(ring + e, 4)
        return (r // 2) * 16 + z, lax.rem(r, 2) * 8 + lax.rem(me, 8)

    def near(e):
        return yh * 16 + za * 4 + lax.rem(zb + e, 4), me

    def across(e):
        return (1 - yh) * 16 + za * 4 + lax.rem(zb + e, 4), me

    def far(e):
        return yh * 16 + lax.rem(za + e, 4) * 4 + zb, me

    wo_rows = pl.ds(_al(lax.rem(me, 8) * 64, 16), 64)
    my_tok = pl.ds(_al(lax.rem(me, 8) * 80, 16), 80)
    barrier = pltpu.get_barrier_semaphore()
    greet = [(dp, lax.rem(me + d, 16)) for d in range(1, 16)]
    greet += [near(e) for e in (1, 2, 3)] + [far(e) for e in (1, 2, 3)] + [across(e) for e in range(4)]
    greet += [((1 - yh) * 16 + z, (1 - y) * 8 + lax.rem(me, 8))]
    loads = [
        pltpu.make_async_copy(src, dst, ld.at[i])
        for i, (src, dst) in enumerate(
            [(bases_hbm, bases_ref), (embed_hbm, embed_ref)]
            + [(convt_hbm.at[96 * j : 96 * j + 96], wcat.at[128 * j : 128 * j + 96]) for j in range(5)]
            + [(qkvt_hbm, qkvt_ref), (gain_hbm, gain_ref), (convb_hbm, convb_ref)]
            + [(wo_hbm, wof.at[wo_rows]), (cot_hbm, cotr.at[my_tok])]
        )
    ]
    for cp in loads:
        cp.start()
    for to in greet:
        pl.semaphore_signal(barrier, inc=1, device_id=to, device_id_type=MESH)
    loads[0].wait()
    ball[pl.ds(_al(me * 80, 16), 80), :] = bases_ref[...].astype(F32).astype(BF)
    pl.semaphore_wait(barrier, len(greet))

    plane = [(0, 1), (0, 3), (1, 0), (1, 1), (1, 3), (0, 2), (1, 2)]

    def ball_of(dev):
        return ball.at[pl.ds(_al(dev * 80, 16), 80)]

    def ysel(dy):
        return y + dy - 2 * dy * y

    bplane = []
    for i, (dy, dx) in enumerate(plane):
        cp = rcopy(ball_of(me), ball_of(me), ss_b.at[i], rs_b.at[i], ctx(ysel(dy), x + dx, core))
        cp.start()
        bplane.append(cp)
    bsib = [rcopy(ball_of(me), ball_of(me), ss_b.at[7], rs_b.at[7], sib)]
    bsib[0].start()

    for j in range(6):
        wcat[128 * j + 96 : 128 * j + 128, :] = jnp.zeros((32, 1536), BF)
    r = lax.broadcasted_iota(jnp.int32, (96, 1536), 0) + 96 * me
    cc = lax.broadcasted_iota(jnp.int32, (96, 1536), 1)
    wcat[640:736, :] = jnp.where(r == cc, 1.0, 0.0).astype(BF)
    for cp in loads[1:7]:
        cp.wait()

    def comp(i, c):
        prod = lax.dot_general(embed_ref[...], wcat[pl.ds(_al(i * 256, 256), 256), :], (((1,), (1,)), ((), ())),
                               preferred_element_type=F32)
        wc[2 * i] = prod[:, 0:128]
        wc[2 * i + 1] = prod[:, 128:256]
        return c

    lax.fori_loop(0, 2, comp, 0)
    for i, (dy, dx) in enumerate(plane):
        bplane[i].wait_recv()
        src = ball_of(ctx(ysel(dy), x + 4 - dx, core))
        cp = rcopy(src, src, ss_b.at[8 + i], rs_b.at[8 + i], sib)
        cp.start()
        bsib.append(cp)

    for cp in loads[7:12]:
        cp.wait()

    cots = []

    def send_cot(d):
        for cc in range(2):
            cols = slice(768 * cc, 768 * cc + 768)
            cp = rcopy(cotr.at[my_tok, cols], cotr.at[my_tok, cols], ss_c.at[2 * d - 2 + cc], rs_c.at[2 * d - 2 + core],
                       ctx(y, x + d, cc))
            cp.start()
            cots.append(cp)

    send_cot(1)
    send_cot(3)

    sends = []
    wrows = pl.ds(_al(core * 192, 16), 192)
    for j in range(12):
        cols = slice(128 * j, 128 * j + 128)
        wt[wrows, cols] = (qkvt_ref[:, cols].astype(F32) * gain_ref[j : j + 1, :]).astype(BF)
    wcopy = rcopy(wt.at[wrows], wt.at[wrows], ss_w, rs_w, sib)
    wcopy.start()
    for cc in range(2):
        cols = slice(768 * cc, 768 * cc + 768)

        @pl.when(core != cc)
        def _():
            rcopy(wof.at[wo_rows, cols], wof.at[wo_rows, cols], ss_o.at[6], rs_o.at[6], sib).start()

    csib = [rcopy(cotr.at[my_tok], cotr.at[my_tok], ss_d.at[0], rs_d.at[0], sib)]
    csib[0].start()

    lax.fori_loop(2, 3, comp, 0)
    for b in range(4):
        for j in range(6):
            wcp[128 * b : 128 * b + 128, 128 * j : 128 * j + 128] = wc[j, pl.ds(b, 128, stride=4), :].astype(BF)
    yb[0:8, :] = jnp.zeros((8, 768), F32)
    yb[1288:1296, :] = jnp.zeros((8, 768), F32)
    bsc[...] = jnp.zeros((8, 128), F32)
    bsc[0:1, 0:96] = convb_ref[...]
    for cp in bsib:
        cp.wait_recv()

    def taps(i, c):
        rows = pl.ds(_al(i * 256, 256), 256)
        bb = ball[rows, :].astype(F32)
        for b in range(4):
            oh[:, 128 * b : 128 * b + 128] = jnp.where(bb == float(b), 1.0, 0.0).astype(BF)
        yb[pl.ds(_al(i * 256 + 8, 8), 256), :] = _dot(oh[...], wcp[...])
        return c


    bias = jnp.broadcast_to(bsc[0:1, :], (128, 128)).T[0:96]

    def act(q, c):
        win = pl.ds(_al(q * 128, 8), 144)
        pre = jnp.zeros((128, 128), F32)
        for j in range(5):
            pre = pre + yb[win, 128 * j : 128 * j + 128][6 + j : 134 + j]
        own = yb[pl.ds(_al(q * 128 + 8, 8), 128), 640:768]
        val = own.T[0:96] + _gelu(pre.T[0:96] + bias)
        st[q // 5, :, pl.ds(_al(lax.rem(q, 5) * 128, 128), 128)] = val.astype(BF)
        return c

    own_rows = pl.ds(_al(me * 96, 16), 96)

    pieces = (slice(0, LA), slice(LA, 640))

    def s1(rel, ct, p):
        to = ctx(y, x + rel + 1, ct) if rel < 3 else ctx(1 - y, x, ct)
        lanes = pieces[p]
        return rcopy(st.at[ct, :, lanes], xt.at[own_rows, lanes], ss1.at[(rel * 2 + ct) * 2 + p],
                     rs1.at[(rel * 2 + core) * 2 + p], to)

    def s1_sib(half, p):
        lanes = pieces[p]
        return rcopy(st.at[half, :, lanes], xt.at[own_rows, lanes], ss1.at[16 + p], rs1.at[16 + p], sib)

    for half in range(2):
        for p, t0, t1, q0, q1 in (
            (0, 3 * half, 2 + 2 * half, 5 * half, 5 * half + 2),
            (1, 2 + 2 * half, 3 + 2 * half, 5 * half + 2, 5 * half + 5),
        ):
            lax.fori_loop(t0, t1, taps, 0)
            lax.fori_loop(q0, q1, act, 0)
            for rel in (3, 0, 2):
                cp = s1(rel, half, p)
                cp.start()
                sends.append(cp)

            @pl.when(core == half)
            def _():
                xt[own_rows, pieces[p]] = st[half, :, pieces[p]]

            @pl.when(core != half)
            def _():
                s1_sib(half, p).start()

    def chip_rows(kk):
        return pl.ds(_al(kk * 192, 16), 192)

    def s1_wait(rel, p):
        lanes = pieces[p]
        for cs in range(2):
            rcopy(st.at[0, :, lanes], xt.at[own_rows, lanes], ss1.at[0], rs1.at[(rel * 2 + cs) * 2 + p], sib).wait_recv()

    def chip_at(yy, d):
        return yy * 4 + lax.rem(x + d, 4)

    def push(ref, ssem, rsem, to):
        cp = rcopy(ref, ref, ssem, rsem, to)
        cp.start()
        sends.append(cp)

    def to_y(d):
        push(xt.at[chip_rows(chip_at(y, 4 - d)), 0:LA], ss2.at[d - 1], rs2.at[d - 1], ctx(1 - y, x, core))

    def half_rows(kk, i):
        return pl.ds(_al(kk * 192 + 96 * i, 16), 96)

    for i, d in ((0, 1), (1, 3)):
        s1_wait(d - 1, 0)
        to_y(d)
        push(xt.at[half_rows(chip_at(y, 4 - d), i), pieces[0]], ss3.at[i], rs3.at[i], ctx(y, x + d, core))
    s1_wait(3, 1)
    for d in (1, 3):
        push(xt.at[chip_rows(chip_at(1 - y, 0)), LA:640], ss2.at[2 + d], rs2.at[2 + d], ctx(y, x + d, core))
    for i, d in ((0, 1), (1, 3)):
        s1_wait(d - 1, 1)
        push(xt.at[half_rows(chip_at(y, 4 - d), i), pieces[1]], ss3.at[2 + i], rs3.at[2 + i], ctx(y, x + d, core))

    def s3_wait(p):
        for i in range(2):
            src = xt.at[own_rows, pieces[p]]
            rcopy(src, src, ss3.at[0], rs3.at[2 * p + i], sib).wait_recv()

    s3_wait(0)
    to_y(2)
    for i, d in ((0, 1), (1, 3)):
        src = xt.at[chip_rows(0), LA:640]
        rcopy(src, src, ss2.at[2 + d], rs2.at[2 + d], sib).wait_recv()
        push(xt.at[half_rows(chip_at(1 - y, 4 - d), i), LA:640], ss4.at[i], rs4.at[i], ctx(y, x + d, core))

    core_cols = pl.ds(_al(core * 768, 128), 768)

    def cot_rows(d, i, n):
        return pl.ds(_al(lax.rem(x + 4 - d, 4) * 160 + 80 * i, 16), n)

    def cot_to_sib(d):
        part = cotr.at[cot_rows(d, 0, 160), core_cols]
        cp = rcopy(part, part, ss_d.at[d], rs_d.at[d], sib)
        cp.start()
        csib.append(cp)

    for i, d in ((0, 1), (1, 3)):
        for cs in range(2):
            rcopy(cotr.at[my_tok, 0:768], cotr.at[my_tok, 0:768], ss_c.at[0], rs_c.at[2 * d - 2 + cs], sib).wait_recv()
        part = cotr.at[cot_rows(d, i, 80), core_cols]
        cp = rcopy(part, part, ss_c.at[2 + i], rs_c.at[2 + i], ctx(y, x + d, core))
        cp.start()
        cots.append(cp)
        cot_to_sib(d)
    for d in (1, 3, 2):
        for cc in range(2):
            part = wof.at[wo_rows, 768 * cc : 768 * cc + 768]
            cp = rcopy(part, part, ss_o.at[2 * d - 2 + cc], rs_o.at[2 * d - 2 + core], ctx(y, x + d, cc))
            cp.start()
            sends.append(cp)

    wcopy.wait()
    for p in range(2):
        s1_sib(0, p).wait_recv()
    s3_wait(1)
    s1_wait(3, 0)

    def sq(i, tot):
        v = xt[pl.ds(_al(i * 128, 128), 128), :].astype(F32)
        return tot + jnp.sum((v * v).reshape(16, 8, 640), axis=0)

    def part(h, lo, hi, row):
        return _dot(wt[192 * h + lo : 192 * h + hi, pl.ds(_al(row * 768, 128), 768)], xt[pl.ds(_al(row * 768, 16), 768), :])

    total = lax.fori_loop(y * 6, y * 6 + 6, sq, jnp.zeros((8, 640), F32))
    for h in range(2):
        acc[h] = part(h, 0, 192, y)
    for d in (1, 3, 2):
        src = xt.at[chip_rows(0), 0:LA]
        rcopy(src, src, ss2.at[d - 1], rs2.at[d - 1], sib).wait_recv()
    for i in range(2):
        src = xt.at[own_rows, LA:640]
        rcopy(src, src, ss4.at[i], rs4.at[i], sib).wait_recv()
    total = lax.fori_loop(6 - y * 6, 12 - y * 6, sq, total)
    scale = lax.rsqrt(jnp.sum(total, axis=0, keepdims=True) * (1.0 / 1536.0) + 1e-06)
    kcopy = []
    for h in range(2):
        kv[core, h] = ((acc[h, 64:192] + part(h, 64, 192, 1 - y)) * scale).astype(BF)
        cp = rcopy(kv.at[core, h], kv.at[core, h], ss_k.at[h], rs_k.at[h], sib)
        cp.start()
        kcopy.append(cp)
    for h in range(2):
        qt[h] = ((acc[h, 0:64] + part(h, 0, 64, 1 - y)) * scale * 0.125).astype(BF)

    scopy = rcopy(sbuf.at[1 - core], sown, ss_s, rs_s, sib)

    @pl.when(core == y)
    def _():
        r = lax.broadcasted_iota(jnp.int32, (160, 640), 0) + 160 * x
        cidx = lax.broadcasted_iota(jnp.int32, (160, 640), 1)
        pick = jnp.where(r == cidx, 1.0, 0.0).astype(BF)
        for n in range(6):
            sbuf[n // 3, :, 256 * (n % 3) : 256 * (n % 3) + 256] = lax.dot_general(
                pick, xt[256 * n : 256 * n + 256, :], (((1,), (1,)), ((), ())), preferred_element_type=F32).astype(BF)
        sown[...] = sbuf[core]
        scopy.start()

    for cp in kcopy:
        cp.wait()
    for h in range(2):
        for half in range(2):
            ks[h, 640 * half : 640 * half + 640, :] = kv[half, h, 0:64, :].astype(F32).T.astype(BF)

    steps = [(h, a, w) for a, w in ((0, 256), (256, 256), (512, 128)) for h in range(2)]

    def score(n):
        h, a, w = steps[n]
        sc[n % 2, :, 0:w] = _dot(ks[h], qt[h, :, a : a + w])

    kx = core * 4 + x
    trows = pl.ds(_al(y * 64, 16), 64)
    tiles = ((0, 256), (256, 256), (512, 128))

    def tcopy(t, cc):
        a, w = tiles[t]
        return rcopy(at.at[64 * cc : 64 * cc + 64, a : a + w], ath.at[trows, a : a + w], ss_t.at[2 * t + cc],
                     rs_t.at[2 * t + y], kx * 2 + cc)

    def acopy(d, cc):
        return rcopy(an.at[pl.ds(_al(lax.rem(x + d, 4) * 160, 16), 160)], aown.at[a_rows, a_cols], ss_a.at[2 * d + cc],
                     rs_a.at[2 * d + core], ctx(y, x + d, cc))

    a_rows = pl.ds(_al(core * 160, 16), 160)
    a_cols = pl.ds(_al(x * 128, 128), 128)

    score(0)
    outs = [None, None]
    for n, (h, a, w) in enumerate(steps):
        if n + 1 < len(steps):
            score(n + 1)
        s = sc[n % 2, :, 0:w]
        p = jnp.exp(s - jnp.max(s, axis=0, keepdims=True))
        den = jnp.sum(p, axis=0, keepdims=True)
        pb = p.astype(BF)
        o = (_dot(kv[0, h, 64:128, :], pb[0:640]) + _dot(kv[1, h, 64:128, :], pb[640:1280])) / den
        at[64 * h : 64 * h + 64, a : a + w] = o.astype(BF)
        outs[h] = o
        if h == 1:
            t = n // 2
            for cc in range(2):
                @pl.when(kx * 2 + cc == me)
                def _():
                    ath[trows, a : a + w] = at[64 * cc : 64 * cc + 64, a : a + w]

                @pl.when(kx * 2 + cc != me)
                def _():
                    tcopy(t, cc).start()
            an[a : a + w, :] = jnp.concatenate(outs, axis=0).T.astype(BF)

    aown[a_rows, a_cols] = an[pl.ds(_al(x * 160, 16), 160), :]
    for d in (1, 3, 2):
        for cc in range(2):
            acopy(d, cc).start()
    for cc in range(2):
        @pl.when(core != cc)
        def _():
            acopy(0, cc).start()

    for i in range(2):
        rcopy(cotr.at[my_tok, 0:768], cotr.at[my_tok, 0:768], ss_c.at[0], rs_c.at[2 + i], sib).wait_recv()
    cot_to_sib(2)

    def t_wait(yy):
        for t in range(3):
            a, w = tiles[t]
            rcopy(at.at[0:64, a : a + w], ath.at[0:64, a : a + w], ss_t.at[0], rs_t.at[2 * t + yy], sib).wait_recv()

    t_wait(1 - y)

    @pl.when(core != y)
    def _():
        t_wait(y)

    for cp in csib:
        cp.wait_recv()

    def block(r, i):
        return pl.ds(_al(lax.rem(r, 2) * 64, 16), 64), pl.ds(_al((r // 2) * 768 + 384 * i, 128), 384)

    ysend, nsend, fsend, gsend = [[], []], [[], []], [[], []], [[], []]
    for i in range(2):
        for hh in range(2):
            cols = slice(768 * hh + 384 * i, 768 * hh + 384 * i + 384)
            gl[:, cols] = _dot(ath[...], cotr[:, cols]).astype(BF)
        for e in (1, 3, 2):
            rows, cols = block(lax.rem(ring + e, 4), i)
            k = 3 * i + e - 1
            cp = rcopy(gl.at[rows, cols], yr.at[k], ss_y.at[k], rs_y.at[k], ring_dev(e))
            cp.start()
            ysend[i].append(cp)

    for i in range(2):
        rows, cols = block(ring, i)
        acc = gl[rows, cols].astype(F32)
        for e, cp in zip((1, 3, 2), ysend[i]):
            cp.wait_recv()
            acc = acc + yr[3 * i + e - 1].astype(F32)
        zs[i] = acc.astype(BF)
        for e in (1, 3, 2):
            k = 3 * i + e - 1
            cp = rcopy(zs.at[i, pl.ds(_al(lax.rem(zb + e, 4) * 16, 16), 16)], nr.at[k], ss_n.at[k], rs_n.at[k], near(e))
            cp.start()
            nsend[i].append(cp)
    zrows = pl.ds(_al(zb * 16, 16), 16)
    for i in range(2):
        acc = zs[i, zrows, :].astype(F32)
        for e, cp in zip((1, 3, 2), nsend[i]):
            cp.wait_recv()
            acc = acc + nr[3 * i + e - 1].astype(F32)
        fr[i, za] = acc.astype(BF)
        for e in (2, 1, 3):
            k = 3 * i + e - 1
            cp = rcopy(fr.at[i, za], fr.at[i, za], ss_f.at[k], rs_f.at[k], far(e))
            cp.start()
            fsend[i].append(cp)
    for i in range(7):
        rcopy(wof.at[0:64, 0:768], wof.at[0:64, 0:768], ss_o.at[0], rs_o.at[i], sib).wait_recv()
    for i in range(2, 8):
        rcopy(an.at[0:160], aown.at[0:160, 0:128], ss_a.at[0], rs_a.at[i], sib).wait_recv()
    rcopy(an.at[0:160], aown.at[0:160, 0:128], ss_a.at[0], rs_a.at[1 - core], sib).wait_recv()
    pbuf[...] = _dot(aown[pl.ds(_al((1 - y) * 160, 16), 160), :], wof[:, core_cols]).astype(BF)
    pcopy = rcopy(pbuf, prx, ss_p, rs_p, ctx(1 - y, x, core))
    pcopy.start()
    pown[...] = _dot(aown[pl.ds(_al(y * 160, 16), 160), :], wof[:, core_cols])

    @pl.when(core == y)
    def _():
        scopy.wait_send()

    for cp in sends + bplane + bsib + cots + csib:
        cp.wait_send()
    for i in range(2):
        for cp in ysend[i] + nsend[i]:
            cp.wait_send()
    for p in range(2):
        s1_sib(0, p).wait_send()
    for cc in range(2):
        @pl.when(kx * 2 + cc != me)
        def _():
            for t in range(3):
                tcopy(t, cc).wait_send()
    for d in (1, 3, 2):
        for cc in range(2):
            acopy(d, cc).wait_send()
    for cc in range(2):
        @pl.when(core != cc)
        def _():
            acopy(0, cc).wait_send()
    rcopy(wof.at[wo_rows, 0:768], wof.at[wo_rows, 0:768], ss_o.at[6], rs_o.at[6], sib).wait_send()

    for i in range(2):
        for cp in fsend[i]:
            cp.wait_recv()
        acc = fr[i, 0].astype(F32)
        for q in range(1, 4):
            acc = acc + fr[i, q].astype(F32)
        rc[i] = acc.astype(BF)
        fcols = pl.ds(_al(yh * 768 + 384 * i, 128), 384)
        fb[zrows, fcols] = rc[i]
        for k, to in enumerate([across(e) for e in range(4)] + [near(e) for e in (1, 2, 3)]):
            cp = rcopy(rc.at[i], fb.at[zrows, fcols], ss_g.at[7 * i + k], rs_g.at[7 * i + k], to)
            cp.start()
            gsend[i].append(cp)

    @pl.when(core != y)
    def _():
        scopy.wait_recv()

    pcopy.wait_recv()
    whole = (sown[...].astype(F32) + (pown[...] + prx[...].astype(F32))).astype(BF)
    obuf[0] = whole[0:80]
    obuf[1] = whole[80:160]
    ocopy = rcopy(obuf.at[1 - core], orx, ss_q, rs_q, sib)
    ocopy.start()
    out_ref[:, core_cols] = obuf[core]

    for i in range(2):
        for cp in gsend[i]:
            cp.wait_recv()
    grad_ref[...] = fb[...]
    ocopy.wait_recv()
    out_ref[:, pl.ds(_al(768 - core * 768, 128), 768)] = orx[...]

    for cp in [pcopy, ocopy]:
        cp.wait_send()
    for i in range(2):
        for cp in fsend[i] + gsend[i]:
            cp.wait_send()


def place_kernel(a_ref, b_ref, oa_ref, ob_ref):
    oa_ref[...] = a_ref[...]
    ob_ref[...] = b_ref[...]


def per_device(bases, embed_w, conv_w, conv_b, norm_g, qkv_w, wo, cotangent):
    vm = pl.BlockSpec(memory_space=pltpu.VMEM)
    V = pltpu.VMEM

    def sems(n):
        return [pltpu.SemaphoreType.DMA((n,)), pltpu.SemaphoreType.DMA((n,))]

    one = [pltpu.SemaphoreType.DMA, pltpu.SemaphoreType.DMA]
    out, wo_grad = pl.pallas_call(
        layer_kernel,
        out_shape=(jax.ShapeDtypeStruct((80, 1536), BF), jax.ShapeDtypeStruct((64, 1536), BF)),
        in_specs=[pl.BlockSpec(memory_space=pltpu.HBM)] * 8,
        out_specs=(vm,) * 2,
        scratch_shapes=[
            V((1280, 128), BF), V((8, 128), F32), V((768, 1536), BF), V((6, 512, 128), F32), V((512, 768), BF),
            V((256, 512), BF), V((1296, 768), F32), V((2, 96, 640), BF), V((1536, 640), BF), V((384, 1536), BF),
            V((2, 64, 640), BF), V((2, 2, 128, 640), BF), V((2, 1280, 64), BF), V((2, 1280, 256), F32),
            V((128, 640), BF), V((640, 128), BF), V((128, 640), BF), V((320, 512), BF), V((2, 160, 768), BF),
            V((160, 768), BF), V((640, 1536), BF), V((512, 1536), BF),
            V((160, 768), BF), V((160, 768), BF), V((160, 768), F32), V((2, 80, 768), BF), V((80, 768), BF),
            V((128, 1536), BF), V((6, 64, 384), BF), V((2, 64, 384), BF), V((6, 16, 384), BF), V((2, 4, 16, 384), BF),
            V((2, 16, 384), BF), V((64, 1536), BF), V((2, 192, 640), F32),
            V((80, 128), jnp.int32), V((512, 1536), BF), V((1, 96), F32), V((192, 1536), BF), V((12, 128), F32),
            pltpu.SemaphoreType.DMA((12,)),
        ] + sems(15) + one + sems(18) + sems(6) + sems(6) + sems(2) + one + sems(6) + sems(8) + sems(4) + sems(7) + one + one
        + sems(4) + sems(2) + sems(6) + sems(6) + sems(6) + sems(14),
        compiler_params=pltpu.CompilerParams(collective_id=0, has_side_effects=True, vmem_limit_bytes=56 << 20),
        name="layer",
    )(bases.reshape(80, 128), embed_w, conv_w.transpose(0, 2, 1).reshape(480, 1536), conv_b[None], qkv_w.T,
      norm_g.reshape(12, 128), wo, cotangent[0])
    out, wo_grad = pl.pallas_call(
        place_kernel,
        out_shape=(jax.ShapeDtypeStruct((80, 1536), BF), jax.ShapeDtypeStruct((64, 1536), BF)),
        in_specs=[vm] * 2,
        out_specs=(vm,) * 2,
        name="place",
    )(out, wo_grad)
    return out[None], wo_grad


def solution(mesh):
    return jax.shard_map(
        per_device,
        mesh=mesh,
        in_specs=(
            P("dp", "ctx"), P(), P(None, None, "ctx"), P("ctx"), P(), P(None, "ctx"), P("ctx", None),
            P("dp", "ctx", None),
        ),
        out_specs=(P("dp", "ctx", None), P("ctx", None)),
        check_vma=False,
    )
```

```python
import functools

import jax
import jax.numpy as jnp
from jax import lax
from jax.experimental import pallas as pl
from jax.experimental.pallas import tpu as pltpu
from jax.sharding import PartitionSpec as P

MESH = pl.DeviceIdType.MESH
BF = jnp.bfloat16
F32 = jnp.float32
LA = 256


def _al(v, m):
    return pl.multiple_of(v, m)


def _dot(a, b):
    return jnp.dot(a, b, preferred_element_type=F32)


def _gelu(v):
    return 0.5 * v * (1.0 + jnp.tanh(0.7978845608028654 * (v + 0.044715 * (v * v * v))))


def layer_kernel(
    bases_hbm, embed_hbm, convt_hbm, convb_hbm, qkvt_hbm, gain_hbm, wo_hbm, cot_hbm,
    out_ref, grad_ref,
    ball, bsc, wcat, wc, wcp, oh, yb, st, xt, wt, qt, kv, ks, sc, at, an, ath, aown, sbuf, sown, cotr, wof,
    pbuf, prx, pown, obuf, orx,
    gl, yr, zs, nr, fr, rc, fb, acc, bases_ref, embed_ref, convb_ref, qkvt_ref, gain_ref, ld,
    ss_b, rs_b, ss_w, rs_w, ss1, rs1, ss2, rs2, ss_c, rs_c, ss_k, rs_k, ss_s, rs_s, ss_t, rs_t, ss_a, rs_a,
    ss_d, rs_d, ss_o, rs_o, ss_p, rs_p, ss_q, rs_q, ss3, rs3, ss4, rs4, ss_y, rs_y, ss_n, rs_n, ss_f, rs_f, ss_g, rs_g,
):
    dp = lax.axis_index("dp")
    me = lax.axis_index("ctx")
    yh, z = dp // 16, lax.rem(dp, 16)
    za, zb = z // 4, lax.rem(z, 4)
    core = lax.rem(me, 2)
    chip = me // 2
    x = lax.rem(chip, 4)
    y = me // 8
    sib = me + 1 - 2 * core
    ring = 2 * yh + y

    def ctx(yy, xx, cc):
        return (yy * 4 + lax.rem(xx, 4)) * 2 + cc

    def rcopy(src, dst, ssem, rsem, to):
        return pltpu.make_async_remote_copy(
            src_ref=src, dst_ref=dst, send_sem=ssem, recv_sem=rsem,
            device_id=to if isinstance(to, tuple) else (dp, to), device_id_type=MESH,
        )

    def ring_dev(e):
        r = lax.rem(ring + e, 4)
        return (r // 2) * 16 + z, lax.rem(r, 2) * 8 + lax.rem(me, 8)

    def near(e):
        return yh * 16 + za * 4 + lax.rem(zb + e, 4), me

    def across(e):
        return (1 - yh) * 16 + za * 4 + lax.rem(zb + e, 4), me

    def far(e):
        return yh * 16 + lax.rem(za + e, 4) * 4 + zb, me

    wo_rows = pl.ds(_al(lax.rem(me, 8) * 64, 16), 64)
    my_tok = pl.ds(_al(lax.rem(me, 8) * 80, 16), 80)
    barrier = pltpu.get_barrier_semaphore()
    greet = [(dp, lax.rem(me + d, 16)) for d in range(1, 16)]
    greet += [near(e) for e in (1, 2, 3)] + [far(e) for e in (1, 2, 3)] + [across(e) for e in range(4)]
    greet += [((1 - yh) * 16 + z, (1 - y) * 8 + lax.rem(me, 8))]
    loads = [
        pltpu.make_async_copy(src, dst, ld.at[i])
        for i, (src, dst) in enumerate(
            [(bases_hbm, bases_ref), (embed_hbm, embed_ref)]
            + [(convt_hbm.at[96 * j : 96 * j + 96], wcat.at[128 * j : 128 * j + 96]) for j in range(5)]
            + [(qkvt_hbm, qkvt_ref), (gain_hbm, gain_ref), (convb_hbm, convb_ref)]
            + [(wo_hbm, wof.at[wo_rows]), (cot_hbm, cotr.at[my_tok])]
        )
    ]
    for cp in loads:
        cp.start()
    for to in greet:
        pl.semaphore_signal(barrier, inc=1, device_id=to, device_id_type=MESH)
    loads[0].wait()
    ball[pl.ds(_al(me * 80, 16), 80), :] = bases_ref[...].astype(F32).astype(BF)
    pl.semaphore_wait(barrier, len(greet))

    plane = [(0, 1), (0, 3), (1, 0), (1, 1), (1, 3), (0, 2), (1, 2)]

    def ball_of(dev):
        return ball.at[pl.ds(_al(dev * 80, 16), 80)]

    def ysel(dy):
        return y + dy - 2 * dy * y

    bplane = []
    for i, (dy, dx) in enumerate(plane):
        cp = rcopy(ball_of(me), ball_of(me), ss_b.at[i], rs_b.at[i], ctx(ysel(dy), x + dx, core))
        cp.start()
        bplane.append(cp)
    bsib = [rcopy(ball_of(me), ball_of(me), ss_b.at[7], rs_b.at[7], sib)]
    bsib[0].start()

    for j in range(6):
        wcat[128 * j + 96 : 128 * j + 128, :] = jnp.zeros((32, 1536), BF)
    r = lax.broadcasted_iota(jnp.int32, (96, 1536), 0) + 96 * me
    cc = lax.broadcasted_iota(jnp.int32, (96, 1536), 1)
    wcat[640:736, :] = jnp.where(r == cc, 1.0, 0.0).astype(BF)
    for cp in loads[1:7]:
        cp.wait()

    def comp(i, c):
        prod = lax.dot_general(embed_ref[...], wcat[pl.ds(_al(i * 256, 256), 256), :], (((1,), (1,)), ((), ())),
                               preferred_element_type=F32)
        wc[2 * i] = prod[:, 0:128]
        wc[2 * i + 1] = prod[:, 128:256]
        return c

    lax.fori_loop(0, 3, comp, 0)
    for cp in loads[7:12]:
        cp.wait()

    for b in range(4):
        for j in range(6):
            wcp[128 * b : 128 * b + 128, 128 * j : 128 * j + 128] = wc[j, pl.ds(b, 128, stride=4), :].astype(BF)
    yb[0:8, :] = jnp.zeros((8, 768), F32)
    yb[1288:1296, :] = jnp.zeros((8, 768), F32)
    bsc[...] = jnp.zeros((8, 128), F32)
    bsc[0:1, 0:96] = convb_ref[...]
    for i, (dy, dx) in enumerate(plane):
        bplane[i].wait_recv()
        src = ball_of(ctx(ysel(dy), x + 4 - dx, core))
        cp = rcopy(src, src, ss_b.at[8 + i], rs_b.at[8 + i], sib)
        cp.start()
        bsib.append(cp)

    cots = []

    def send_cot(d):
        for cc in range(2):
            cols = slice(768 * cc, 768 * cc + 768)
            cp = rcopy(cotr.at[my_tok, cols], cotr.at[my_tok, cols], ss_c.at[2 * d - 2 + cc], rs_c.at[2 * d - 2 + core],
                       ctx(y, x + d, cc))
            cp.start()
            cots.append(cp)

    send_cot(1)
    send_cot(3)

    sends = []
    for cp in bsib:
        cp.wait_recv()

    def taps(i, c):
        rows = pl.ds(_al(i * 256, 256), 256)
        bb = ball[rows, :].astype(F32)
        for b in range(4):
            oh[:, 128 * b : 128 * b + 128] = jnp.where(bb == float(b), 1.0, 0.0).astype(BF)
        yb[pl.ds(_al(i * 256 + 8, 8), 256), :] = _dot(oh[...], wcp[...])
        return c


    bias = jnp.broadcast_to(bsc[0:1, :], (128, 128)).T[0:96]

    def act(q, c):
        win = pl.ds(_al(q * 128, 8), 144)
        pre = jnp.zeros((128, 128), F32)
        for j in range(5):
            pre = pre + yb[win, 128 * j : 128 * j + 128][6 + j : 134 + j]
        own = yb[pl.ds(_al(q * 128 + 8, 8), 128), 640:768]
        val = own.T[0:96] + _gelu(pre.T[0:96] + bias)
        st[q // 5, :, pl.ds(_al(lax.rem(q, 5) * 128, 128), 128)] = val.astype(BF)
        return c

    own_rows = pl.ds(_al(me * 96, 16), 96)

    pieces = (slice(0, LA), slice(LA, 640))

    def s1(rel, ct, p):
        to = ctx(y, x + rel + 1, ct) if rel < 3 else ctx(1 - y, x, ct)
        lanes = pieces[p]
        return rcopy(st.at[ct, :, lanes], xt.at[own_rows, lanes], ss1.at[(rel * 2 + ct) * 2 + p],
                     rs1.at[(rel * 2 + core) * 2 + p], to)

    def s1_sib(half, p):
        lanes = pieces[p]
        return rcopy(st.at[half, :, lanes], xt.at[own_rows, lanes], ss1.at[16 + p], rs1.at[16 + p], sib)

    for half in range(2):
        for p, t0, t1, q0, q1 in (
            (0, 3 * half, 2 + 2 * half, 5 * half, 5 * half + 2),
            (1, 2 + 2 * half, 3 + 2 * half, 5 * half + 2, 5 * half + 5),
        ):
            lax.fori_loop(t0, t1, taps, 0)
            lax.fori_loop(q0, q1, act, 0)
            for rel in (3, 0, 2):
                cp = s1(rel, half, p)
                cp.start()
                sends.append(cp)

            @pl.when(core == half)
            def _():
                xt[own_rows, pieces[p]] = st[half, :, pieces[p]]

            @pl.when(core != half)
            def _():
                s1_sib(half, p).start()

    wrows = pl.ds(_al(core * 192, 16), 192)
    for j in range(12):
        cols = slice(128 * j, 128 * j + 128)
        wt[wrows, cols] = (qkvt_ref[:, cols].astype(F32) * gain_ref[j : j + 1, :]).astype(BF)
    wcopy = rcopy(wt.at[wrows], wt.at[wrows], ss_w, rs_w, sib)
    wcopy.start()
    for cc in range(2):
        cols = slice(768 * cc, 768 * cc + 768)

        @pl.when(core != cc)
        def _():
            rcopy(wof.at[wo_rows, cols], wof.at[wo_rows, cols], ss_o.at[6], rs_o.at[6], sib).start()

    csib = [rcopy(cotr.at[my_tok], cotr.at[my_tok], ss_d.at[0], rs_d.at[0], sib)]
    csib[0].start()

    def chip_rows(kk):
        return pl.ds(_al(kk * 192, 16), 192)

    def s1_wait(rel, p):
        lanes = pieces[p]
        for cs in range(2):
            rcopy(st.at[0, :, lanes], xt.at[own_rows, lanes], ss1.at[0], rs1.at[(rel * 2 + cs) * 2 + p], sib).wait_recv()

    def chip_at(yy, d):
        return yy * 4 + lax.rem(x + d, 4)

    def push(ref, ssem, rsem, to):
        cp = rcopy(ref, ref, ssem, rsem, to)
        cp.start()
        sends.append(cp)

    def to_y(d):
        push(xt.at[chip_rows(chip_at(y, 4 - d)), 0:LA], ss2.at[d - 1], rs2.at[d - 1], ctx(1 - y, x, core))

    def half_rows(kk, i):
        return pl.ds(_al(kk * 192 + 96 * i, 16), 96)

    for i, d in ((0, 1), (1, 3)):
        s1_wait(d - 1, 0)
        to_y(d)
        push(xt.at[half_rows(chip_at(y, 4 - d), i), pieces[0]], ss3.at[i], rs3.at[i], ctx(y, x + d, core))
    s1_wait(3, 1)
    for d in (1, 3):
        push(xt.at[chip_rows(chip_at(1 - y, 0)), LA:640], ss2.at[2 + d], rs2.at[2 + d], ctx(y, x + d, core))
    for i, d in ((0, 1), (1, 3)):
        s1_wait(d - 1, 1)
        push(xt.at[half_rows(chip_at(y, 4 - d), i), pieces[1]], ss3.at[2 + i], rs3.at[2 + i], ctx(y, x + d, core))

    def s3_wait(p):
        for i in range(2):
            src = xt.at[own_rows, pieces[p]]
            rcopy(src, src, ss3.at[0], rs3.at[2 * p + i], sib).wait_recv()

    s3_wait(0)
    to_y(2)
    for i, d in ((0, 1), (1, 3)):
        src = xt.at[chip_rows(0), LA:640]
        rcopy(src, src, ss2.at[2 + d], rs2.at[2 + d], sib).wait_recv()
        push(xt.at[half_rows(chip_at(1 - y, 4 - d), i), LA:640], ss4.at[i], rs4.at[i], ctx(y, x + d, core))

    core_cols = pl.ds(_al(core * 768, 128), 768)

    def cot_rows(d, i, n):
        return pl.ds(_al(lax.rem(x + 4 - d, 4) * 160 + 80 * i, 16), n)

    def cot_to_sib(d):
        part = cotr.at[cot_rows(d, 0, 160), core_cols]
        cp = rcopy(part, part, ss_d.at[d], rs_d.at[d], sib)
        cp.start()
        csib.append(cp)

    for i, d in ((0, 1), (1, 3)):
        for cs in range(2):
            rcopy(cotr.at[my_tok, 0:768], cotr.at[my_tok, 0:768], ss_c.at[0], rs_c.at[2 * d - 2 + cs], sib).wait_recv()
        part = cotr.at[cot_rows(d, i, 80), core_cols]
        cp = rcopy(part, part, ss_c.at[2 + i], rs_c.at[2 + i], ctx(y, x + d, core))
        cp.start()
        cots.append(cp)
        cot_to_sib(d)
    wcopy.wait()
    for p in range(2):
        s1_sib(0, p).wait_recv()
    s3_wait(1)
    s1_wait(3, 0)

    def sq(i, tot):
        v = xt[pl.ds(_al(i * 128, 128), 128), :].astype(F32)
        return tot + jnp.sum((v * v).reshape(16, 8, 640), axis=0)

    def part(h, lo, hi, row):
        return _dot(wt[192 * h + lo : 192 * h + hi, pl.ds(_al(row * 768, 128), 768)], xt[pl.ds(_al(row * 768, 16), 768), :])

    total = lax.fori_loop(y * 6, y * 6 + 6, sq, jnp.zeros((8, 640), F32))
    for h in range(2):
        acc[h] = part(h, 0, 192, y)
    for d in (1, 3, 2):
        src = xt.at[chip_rows(0), 0:LA]
        rcopy(src, src, ss2.at[d - 1], rs2.at[d - 1], sib).wait_recv()
    for i in range(2):
        src = xt.at[own_rows, LA:640]
        rcopy(src, src, ss4.at[i], rs4.at[i], sib).wait_recv()
    total = lax.fori_loop(6 - y * 6, 12 - y * 6, sq, total)
    scale = lax.rsqrt(jnp.sum(total, axis=0, keepdims=True) * (1.0 / 1536.0) + 1e-06)
    kcopy = []
    for h in range(2):
        kv[core, h] = ((acc[h, 64:192] + part(h, 64, 192, 1 - y)) * scale).astype(BF)
        cp = rcopy(kv.at[core, h], kv.at[core, h], ss_k.at[h], rs_k.at[h], sib)
        cp.start()
        kcopy.append(cp)
    for h in range(2):
        qt[h] = ((acc[h, 0:64] + part(h, 0, 64, 1 - y)) * scale * 0.125).astype(BF)

    for d in (1, 3):
        for cc in range(2):
            part = wof.at[wo_rows, 768 * cc : 768 * cc + 768]
            cp = rcopy(part, part, ss_o.at[2 * d - 2 + cc], rs_o.at[2 * d - 2 + core], ctx(y, x + d, cc))
            cp.start()
            sends.append(cp)

    scopy = rcopy(sbuf.at[1 - core], sown, ss_s, rs_s, sib)

    @pl.when(core == y)
    def _():
        r = lax.broadcasted_iota(jnp.int32, (160, 640), 0) + 160 * x
        cidx = lax.broadcasted_iota(jnp.int32, (160, 640), 1)
        pick = jnp.where(r == cidx, 1.0, 0.0).astype(BF)
        for n in range(6):
            sbuf[n // 3, :, 256 * (n % 3) : 256 * (n % 3) + 256] = lax.dot_general(
                pick, xt[256 * n : 256 * n + 256, :], (((1,), (1,)), ((), ())), preferred_element_type=F32).astype(BF)
        sown[...] = sbuf[core]
        scopy.start()

    for cp in kcopy:
        cp.wait()
    for h in range(2):
        for half in range(2):
            ks[h, 640 * half : 640 * half + 640, :] = kv[half, h, 0:64, :].astype(F32).T.astype(BF)

    steps = [(h, a, w) for a, w in ((0, 256), (256, 256), (512, 128)) for h in range(2)]

    def score(n):
        h, a, w = steps[n]
        sc[n % 2, :, 0:w] = _dot(ks[h], qt[h, :, a : a + w])

    kx = core * 4 + x
    trows = pl.ds(_al(y * 64, 16), 64)
    tiles = ((0, 256), (256, 256), (512, 128))

    def tcopy(t, cc):
        a, w = tiles[t]
        return rcopy(at.at[64 * cc : 64 * cc + 64, a : a + w], ath.at[trows, a : a + w], ss_t.at[2 * t + cc],
                     rs_t.at[2 * t + y], kx * 2 + cc)

    def acopy(d, cc):
        return rcopy(an.at[pl.ds(_al(lax.rem(x + d, 4) * 160, 16), 160)], aown.at[a_rows, a_cols], ss_a.at[2 * d + cc],
                     rs_a.at[2 * d + core], ctx(y, x + d, cc))

    a_rows = pl.ds(_al(core * 160, 16), 160)
    a_cols = pl.ds(_al(x * 128, 128), 128)

    score(0)
    outs = [None, None]
    for n, (h, a, w) in enumerate(steps):
        if n + 1 < len(steps):
            score(n + 1)
        s = sc[n % 2, :, 0:w]
        p = jnp.exp(s - jnp.max(s, axis=0, keepdims=True))
        den = jnp.sum(p, axis=0, keepdims=True)
        pb = p.astype(BF)
        o = (_dot(kv[0, h, 64:128, :], pb[0:640]) + _dot(kv[1, h, 64:128, :], pb[640:1280])) / den
        at[64 * h : 64 * h + 64, a : a + w] = o.astype(BF)
        outs[h] = o
        if h == 1:
            t = n // 2
            for cc in range(2):
                @pl.when(kx * 2 + cc == me)
                def _():
                    ath[trows, a : a + w] = at[64 * cc : 64 * cc + 64, a : a + w]

                @pl.when(kx * 2 + cc != me)
                def _():
                    tcopy(t, cc).start()

    for i in range(2):
        rcopy(cotr.at[my_tok, 0:768], cotr.at[my_tok, 0:768], ss_c.at[0], rs_c.at[2 + i], sib).wait_recv()
    cot_to_sib(2)

    def t_wait(yy):
        for t in range(3):
            a, w = tiles[t]
            rcopy(at.at[0:64, a : a + w], ath.at[0:64, a : a + w], ss_t.at[0], rs_t.at[2 * t + yy], sib).wait_recv()

    t_wait(1 - y)

    @pl.when(core != y)
    def _():
        t_wait(y)

    for cp in csib:
        cp.wait_recv()

    def block(r, i):
        return pl.ds(_al(lax.rem(r, 2) * 64, 16), 64), pl.ds(_al((r // 2) * 768 + 384 * i, 128), 384)

    ysend, nsend, fsend, gsend = [[], []], [[], []], [[], []], [[], []]
    for i in range(2):
        for hh in range(2):
            cols = slice(768 * hh + 384 * i, 768 * hh + 384 * i + 384)
            gl[:, cols] = _dot(ath[...], cotr[:, cols]).astype(BF)
        for e in (1, 3, 2):
            rows, cols = block(lax.rem(ring + e, 4), i)
            k = 3 * i + e - 1
            cp = rcopy(gl.at[rows, cols], yr.at[k], ss_y.at[k], rs_y.at[k], ring_dev(e))
            cp.start()
            ysend[i].append(cp)

    def o_wait(i):
        rcopy(wof.at[0:64, 0:768], wof.at[0:64, 0:768], ss_o.at[0], rs_o.at[i], sib).wait_recv()

    for i, d in ((0, 1), (1, 3)):
        for cs in range(2):
            o_wait(2 * d - 2 + cs)
        part = wof.at[pl.ds(_al((lax.rem(x + 4 - d, 4) * 2 + i) * 64, 16), 64), core_cols]
        cp = rcopy(part, part, ss_o.at[2 + i], rs_o.at[2 + i], ctx(y, x + d, core))
        cp.start()
        sends.append(cp)

    an[...] = at[...].astype(F32).T.astype(BF)

    aown[a_rows, a_cols] = an[pl.ds(_al(x * 160, 16), 160), :]
    for d in (1, 3, 2):
        for cc in range(2):
            acopy(d, cc).start()
    for cc in range(2):
        @pl.when(core != cc)
        def _():
            acopy(0, cc).start()

    for i in range(2):
        rows, cols = block(ring, i)
        acc = gl[rows, cols].astype(F32)
        for e, cp in zip((1, 3, 2), ysend[i]):
            cp.wait_recv()
            acc = acc + yr[3 * i + e - 1].astype(F32)
        zs[i] = acc.astype(BF)
        for e in (1, 3, 2):
            k = 3 * i + e - 1
            cp = rcopy(zs.at[i, pl.ds(_al(lax.rem(zb + e, 4) * 16, 16), 16)], nr.at[k], ss_n.at[k], rs_n.at[k], near(e))
            cp.start()
            nsend[i].append(cp)
    zrows = pl.ds(_al(zb * 16, 16), 16)
    for i in range(2):
        acc = zs[i, zrows, :].astype(F32)
        for e, cp in zip((1, 3, 2), nsend[i]):
            cp.wait_recv()
            acc = acc + nr[3 * i + e - 1].astype(F32)
        fr[i, za] = acc.astype(BF)
        for e in (2, 1, 3):
            k = 3 * i + e - 1
            cp = rcopy(fr.at[i, za], fr.at[i, za], ss_f.at[k], rs_f.at[k], far(e))
            cp.start()
            fsend[i].append(cp)
    for i in (2, 3, 6):
        o_wait(i)
    for i in range(2, 8):
        rcopy(an.at[0:160], aown.at[0:160, 0:128], ss_a.at[0], rs_a.at[i], sib).wait_recv()
    rcopy(an.at[0:160], aown.at[0:160, 0:128], ss_a.at[0], rs_a.at[1 - core], sib).wait_recv()
    pbuf[...] = _dot(aown[pl.ds(_al((1 - y) * 160, 16), 160), :], wof[:, core_cols]).astype(BF)
    pcopy = rcopy(pbuf, prx, ss_p, rs_p, ctx(1 - y, x, core))
    pcopy.start()
    pown[...] = _dot(aown[pl.ds(_al(y * 160, 16), 160), :], wof[:, core_cols])

    @pl.when(core == y)
    def _():
        scopy.wait_send()

    for cp in sends + bplane + bsib + cots + csib:
        cp.wait_send()
    for i in range(2):
        for cp in ysend[i] + nsend[i]:
            cp.wait_send()
    for p in range(2):
        s1_sib(0, p).wait_send()
    for cc in range(2):
        @pl.when(kx * 2 + cc != me)
        def _():
            for t in range(3):
                tcopy(t, cc).wait_send()
    for d in (1, 3, 2):
        for cc in range(2):
            acopy(d, cc).wait_send()
    for cc in range(2):
        @pl.when(core != cc)
        def _():
            acopy(0, cc).wait_send()
    rcopy(wof.at[wo_rows, 0:768], wof.at[wo_rows, 0:768], ss_o.at[6], rs_o.at[6], sib).wait_send()

    for i in range(2):
        for cp in fsend[i]:
            cp.wait_recv()
        acc = fr[i, 0].astype(F32)
        for q in range(1, 4):
            acc = acc + fr[i, q].astype(F32)
        rc[i] = acc.astype(BF)
        fcols = pl.ds(_al(yh * 768 + 384 * i, 128), 384)
        fb[zrows, fcols] = rc[i]
        for k, to in enumerate([across(e) for e in range(4)] + [near(e) for e in (1, 2, 3)]):
            cp = rcopy(rc.at[i], fb.at[zrows, fcols], ss_g.at[7 * i + k], rs_g.at[7 * i + k], to)
            cp.start()
            gsend[i].append(cp)

    @pl.when(core != y)
    def _():
        scopy.wait_recv()

    pcopy.wait_recv()
    whole = (sown[...].astype(F32) + (pown[...] + prx[...].astype(F32))).astype(BF)
    obuf[0] = whole[0:80]
    obuf[1] = whole[80:160]
    ocopy = rcopy(obuf.at[1 - core], orx, ss_q, rs_q, sib)
    ocopy.start()
    out_ref[:, core_cols] = obuf[core]

    for i in range(2):
        for cp in gsend[i]:
            cp.wait_recv()
    grad_ref[...] = fb[...]
    ocopy.wait_recv()
    out_ref[:, pl.ds(_al(768 - core * 768, 128), 768)] = orx[...]

    for cp in [pcopy, ocopy]:
        cp.wait_send()
    for i in range(2):
        for cp in fsend[i] + gsend[i]:
            cp.wait_send()


def place_kernel(a_ref, b_ref, oa_ref, ob_ref):
    oa_ref[...] = a_ref[...]
    ob_ref[...] = b_ref[...]


def per_device(bases, embed_w, conv_w, conv_b, norm_g, qkv_w, wo, cotangent):
    vm = pl.BlockSpec(memory_space=pltpu.VMEM)
    V = pltpu.VMEM

    def sems(n):
        return [pltpu.SemaphoreType.DMA((n,)), pltpu.SemaphoreType.DMA((n,))]

    one = [pltpu.SemaphoreType.DMA, pltpu.SemaphoreType.DMA]
    out, wo_grad = pl.pallas_call(
        layer_kernel,
        out_shape=(jax.ShapeDtypeStruct((80, 1536), BF), jax.ShapeDtypeStruct((64, 1536), BF)),
        in_specs=[pl.BlockSpec(memory_space=pltpu.HBM)] * 8,
        out_specs=(vm,) * 2,
        scratch_shapes=[
            V((1280, 128), BF), V((8, 128), F32), V((768, 1536), BF), V((6, 512, 128), F32), V((512, 768), BF),
            V((256, 512), BF), V((1296, 768), F32), V((2, 96, 640), BF), V((1536, 640), BF), V((384, 1536), BF),
            V((2, 64, 640), BF), V((2, 2, 128, 640), BF), V((2, 1280, 64), BF), V((2, 1280, 256), F32),
            V((128, 640), BF), V((640, 128), BF), V((128, 640), BF), V((320, 512), BF), V((2, 160, 768), BF),
            V((160, 768), BF), V((640, 1536), BF), V((512, 1536), BF),
            V((160, 768), BF), V((160, 768), BF), V((160, 768), F32), V((2, 80, 768), BF), V((80, 768), BF),
            V((128, 1536), BF), V((6, 64, 384), BF), V((2, 64, 384), BF), V((6, 16, 384), BF), V((2, 4, 16, 384), BF),
            V((2, 16, 384), BF), V((64, 1536), BF), V((2, 192, 640), F32),
            V((80, 128), jnp.int32), V((512, 1536), BF), V((1, 96), F32), V((192, 1536), BF), V((12, 128), F32),
            pltpu.SemaphoreType.DMA((12,)),
        ] + sems(15) + one + sems(18) + sems(6) + sems(6) + sems(2) + one + sems(6) + sems(8) + sems(4) + sems(7) + one + one
        + sems(4) + sems(2) + sems(6) + sems(6) + sems(6) + sems(14),
        compiler_params=pltpu.CompilerParams(collective_id=0, has_side_effects=True, vmem_limit_bytes=56 << 20),
        name="layer",
    )(bases.reshape(80, 128), embed_w, conv_w.transpose(0, 2, 1).reshape(480, 1536), conv_b[None], qkv_w.T,
      norm_g.reshape(12, 128), wo, cotangent[0])
    out, wo_grad = pl.pallas_call(
        place_kernel,
        out_shape=(jax.ShapeDtypeStruct((80, 1536), BF), jax.ShapeDtypeStruct((64, 1536), BF)),
        in_specs=[vm] * 2,
        out_specs=(vm,) * 2,
        name="place",
    )(out, wo_grad)
    return out[None], wo_grad


def solution(mesh):
    return jax.shard_map(
        per_device,
        mesh=mesh,
        in_specs=(
            P("dp", "ctx"), P(), P(None, None, "ctx"), P("ctx"), P(), P(None, "ctx"), P("ctx", None),
            P("dp", "ctx", None),
        ),
        out_specs=(P("dp", "ctx", None), P("ctx", None)),
        check_vma=False,
    )
```
